256 devices in a mesh: seq: 32 (over z, y), head: 8 (over x, core).
Axes of the slice: x: 4, y: 4, z: 8, core: 2. Of those that a mesh axis runs over, the one named last changes fastest.
Arguments:
- queries: bfloat16 [16384, 4096], P('seq', 'head'), may hold values from -6 to 6
- keys: bfloat16 [16384, 4096], P('seq', 'head'), may hold values from -6 to 6
- values: bfloat16 [16384, 4096], P('seq', 'head'), may hold values from -6 to 6
- gate: bfloat16 [16384, 4096], P('seq', 'head'), may hold values from -6 to 6
- log_decay: bfloat16 [16, 16384], P('head', 'seq'), may hold values from -3 to 0
- trunc_blocks: int32 [16], P('head'), may hold values from 2 to 64, as said below
- norm_gain: bfloat16 [4096], P('head'), may hold values from 0.099609375 to 1.8984375
- w_out: bfloat16 [4096, 4096], P('head'), may hold values from -0.09375 to 0.09375
Outputs:
- mixed: bfloat16 [16384, 4096], P(('seq', 'head'))
The draws below stay inside these ranges and needn't reach their ends.
Inputs may be any that keep to these rules, and one draw needn't show every extreme that they name: `trunc_blocks`: each head's value is 2 or 64, and both values occur.
All inputs are finite; a program needn't handle non-finite values.
Results may differ from the reference program's by a relative error of at most 0.02.
Values may be sent and summed in bfloat16 or wider, within the bound.
A program may use at most 64 MiB of HBM per device.

```python
import jax
import jax.numpy as jnp
from jax import lax

D = 4096
RETENTION_HEADS = 16
DH = 256
BLOCK = 256
FAST = 2
SEQUENCE_TOKENS = 16384
NBLK = 64
N_HEAD = 8


def head_kinds(key):
    order = jax.random.permutation(jax.random.fold_in(key, 101), RETENTION_HEADS)
    fast_count = jax.random.randint(jax.random.fold_in(key, 102), (), 1, RETENTION_HEADS)
    return order < fast_count


def draw_trunc_blocks(key, part):
    is_fast = head_kinds(key)
    return jnp.where(is_fast, FAST, NBLK).astype(jnp.int32)


def draw_log_decay(key, part):
    is_fast = head_kinds(key)
    lifetime = jax.random.uniform(jax.random.fold_in(key, 201), (RETENTION_HEADS, 1), jnp.float32, 0.12, 0.2) * BLOCK + 1.0
    long_rate = jax.random.uniform(jax.random.fold_in(key, 202), (RETENTION_HEADS, 1), jnp.float32, 0.2, 0.7) / SEQUENCE_TOKENS
    initial_decay_rate = jnp.where(is_fast[:, None], 1.0 / lifetime, long_rate)
    approximate_value = jnp.exp(jax.random.uniform(jax.random.fold_in(key, 203), (RETENTION_HEADS, SEQUENCE_TOKENS), jnp.float32, -0.7, 0.7))
    sudden_increase = jax.random.uniform(jax.random.fold_in(key, 204), (RETENTION_HEADS, SEQUENCE_TOKENS), jnp.float32) < 3.0 / SEQUENCE_TOKENS
    rate_decrease = jnp.log(jax.random.uniform(jax.random.fold_in(key, 205), (RETENTION_HEADS, SEQUENCE_TOKENS), jnp.float32, 0.5, 0.8))
    decay_rates = -initial_decay_rate * approximate_value + jnp.where(sudden_increase, rate_decrease, 0.0)
    return decay_rates.astype(jnp.bfloat16)


def levels(rng, dims, split, least, high):
    level = 1.0
    for position, parts in split:
        draws = jax.random.uniform(jax.random.fold_in(jax.random.fold_in(rng, 6), position), (parts,), jnp.float32, least / len(split), high / len(split))
        level = level * jnp.repeat(jnp.exp(draws), dims[position] // parts).reshape((-1,) + (1,) * (len(dims) - 1 - position))
    return level


def bell_draw(stream_key, dims, spread, most, pieces=(), kind=jnp.bfloat16):
    level = levels(stream_key, dims, pieces, -0.22, 0.18) if pieces else 1.0
    values = jax.random.normal(stream_key, dims, jnp.float32) * spread * level
    return jnp.minimum(jnp.maximum(values, -most), most).astype(kind)


def setup_inputs(seed: int = 0) -> dict:
    streams_of = jax.random.split(jax.random.key(seed), 9)
    queries = bell_draw(streams_of[0], (SEQUENCE_TOKENS, D), 1.0, 6.0, ((0, 32), (1, 8)))
    keys = bell_draw(streams_of[1], (SEQUENCE_TOKENS, D), 1.0, 6.0, ((0, 32), (1, 8)))
    values = bell_draw(streams_of[2], (SEQUENCE_TOKENS, D), 1.0, 6.0, ((0, 32), (1, 8)))
    gate = bell_draw(streams_of[3], (SEQUENCE_TOKENS, D), 1.0, 6.0, ((0, 32), (1, 8)))
    log_decay = draw_log_decay(jax.random.fold_in(streams_of[8], 71), 0)
    trunc_blocks = draw_trunc_blocks(jax.random.fold_in(streams_of[8], 71), 0)
    norm_gain = jnp.clip(1.0 + 0.18 * jax.random.normal(streams_of[6], (D,), jnp.float32), 0.099609375, 1.8984375).astype(jnp.bfloat16)
    w_out = bell_draw(streams_of[7], (D, D), D ** -0.5, 0.09375, ((0, 8),))
    return dict(queries=queries, keys=keys, values=values, gate=gate, log_decay=log_decay, trunc_blocks=trunc_blocks, norm_gain=norm_gain, w_out=w_out)


def reference(queries, keys, values, gate, log_decay, trunc_blocks, norm_gain, w_out):
    token_count = queries.shape[0]
    query_heads = queries.reshape(token_count, RETENTION_HEADS, DH)
    key_heads = keys.reshape(token_count, RETENTION_HEADS, DH)
    value_heads = values.reshape(token_count, RETENTION_HEADS, DH)
    cumulative = jnp.cumsum(log_decay.astype(jnp.float32), axis=1)
    block_total = token_count // BLOCK
    is_fast = trunc_blocks < block_total
    reach = jnp.where(is_fast, trunc_blocks, 0)
    edge_rows = FAST * BLOCK
    padded_keys = jnp.concatenate([jnp.zeros((edge_rows, RETENTION_HEADS, DH), keys.dtype), key_heads], 0)
    padded_values = jnp.concatenate([jnp.zeros((edge_rows, RETENTION_HEADS, DH), values.dtype), value_heads], 0)
    padded_logs = jnp.concatenate([jnp.zeros((RETENTION_HEADS, edge_rows), jnp.float32), cumulative], 1)
    query_index = jnp.arange(BLOCK, dtype=jnp.int32)
    key_index = jnp.arange(edge_rows + BLOCK, dtype=jnp.int32) - edge_rows
    causal = key_index[None, :] <= query_index[:, None]
    block_gap = query_index[:, None] // BLOCK - key_index[None, :] // BLOCK
    visible = causal[None] & (block_gap[None] <= reach[:, None, None])
    slow_mask = jnp.where(is_fast, 0.0, 1.0).astype(jnp.float32)

    def advance(state, index):
        start = (index * BLOCK).astype(jnp.int32)
        zero = jnp.zeros((), jnp.int32)
        query_block = lax.dynamic_slice(query_heads, (start, zero, zero), (BLOCK, RETENTION_HEADS, DH)).astype(jnp.float32)
        key_block = lax.dynamic_slice(padded_keys, (start, zero, zero), (edge_rows + BLOCK, RETENTION_HEADS, DH)).astype(jnp.float32)
        value_block = lax.dynamic_slice(padded_values, (start, zero, zero), (edge_rows + BLOCK, RETENTION_HEADS, DH)).astype(jnp.float32)
        query_logs = lax.dynamic_slice(cumulative, (zero, start), (RETENTION_HEADS, BLOCK))
        key_logs = lax.dynamic_slice(padded_logs, (zero, start), (RETENTION_HEADS, edge_rows + BLOCK))
        prior_log = lax.dynamic_slice(padded_logs, (zero, start + edge_rows - 1), (RETENTION_HEADS, 1))
        scores = jnp.einsum('thd,shd->hts', query_block, key_block)
        decay = jnp.exp(jnp.minimum(query_logs[:, :, None] - key_logs[:, None, :], 0.0))
        weights = jnp.where(visible, scores * decay, 0.0).astype(jnp.bfloat16)
        weights = lax.optimization_barrier(weights).astype(jnp.float32)
        window = jnp.einsum('hts,shd->thd', weights, value_block)
        carried = jnp.einsum('thd,hde->the', query_block, state, precision=lax.Precision.HIGHEST)
        carried = carried * (jnp.exp(query_logs - prior_log) * slow_mask[:, None]).T[:, :, None]
        end_log = query_logs[:, -1:]
        own_keys = key_block[edge_rows:] * jnp.exp(end_log - query_logs).T[:, :, None]
        own_values = value_block[edge_rows:]
        state = jnp.exp(end_log - prior_log)[:, :, None] * state + jnp.einsum('shd,she->hde', own_keys, own_values, precision=lax.Precision.HIGHEST)
        return (state, window + carried)
    _, blocks = lax.scan(advance, jnp.zeros((RETENTION_HEADS, DH, DH), jnp.float32), jnp.arange(block_total, dtype=jnp.int32))
    retained = blocks.reshape(token_count, RETENTION_HEADS, DH)
    row_mean = lax.optimization_barrier(jnp.mean(retained, axis=-1, keepdims=True))
    centered = retained - row_mean
    row_var = lax.optimization_barrier(jnp.mean(centered * centered, axis=-1, keepdims=True))
    normed = (centered * lax.rsqrt(row_var + 1e-05)).reshape(token_count, RETENTION_HEADS * DH)
    hidden = (normed * norm_gain.astype(jnp.float32) * jax.nn.silu(gate.astype(jnp.float32))).astype(jnp.bfloat16)
    group_rows = RETENTION_HEADS * DH // N_HEAD
    total = jnp.zeros((token_count, w_out.shape[1]), jnp.float32)
    for group in range(N_HEAD):
        partial_sum = jnp.dot(hidden[:, group * group_rows:(group + 1) * group_rows], w_out[group * group_rows:(group + 1) * group_rows], preferred_element_type=jnp.float32).astype(jnp.bfloat16)
        total = total + lax.optimization_barrier(partial_sum).astype(jnp.float32)
    return total.astype(jnp.bfloat16)
```

```python
import functools

import jax
import jax.numpy as jnp
from jax import lax
from jax.experimental import pallas as pl
from jax.experimental.pallas import tpu as pltpu
from jax.sharding import PartitionSpec as P

MESH = pl.DeviceIdType.MESH
F32 = jnp.float32
BF16 = jnp.bfloat16
BLOCK = 256
DH = 256
CHUNK = 512
HALF = CHUNK // 2
PIECE = 64
RING = 4


def nt(a, b):
    return lax.dot_general(a, b, (((1,), (1,)), ((), ())), preferred_element_type=F32)


def tn(a, b):
    return lax.dot_general(a, b, (((0,), (0,)), ((), ())), preferred_element_type=F32)


def nn(a, b):
    return jnp.dot(a, b, preferred_element_type=F32)


def twice(a):
    return jnp.concatenate([a, a], axis=1)


def kernel(
    nseq, nchunk, steps,
    q_hbm, k_hbm, v_hbm, g_hbm, ld_hbm, trunc, gain_hbm, w_hbm,
    out_hbm,
    q, k, v, g, ld, gain, w, w_sib,
    state, first, last, last_in, dec, dec_in, pieces, prefixes, prior,
    ret, gated, grow, hid, mine, theirs, part, passed, direct, summed, out,
    load_sem, dec_sem, one_sem, two_sem, last_sem, wsib_sem, hid_sem, p_send, p_recv, out_sem,
):
    seq, head = lax.axis_index("seq"), lax.axis_index("head")
    x, core = lax.div(head, 2), lax.rem(head, 2)
    right = (seq, lax.rem(x + 1, RING) * 2 + core)
    left = (seq, lax.rem(x + RING - 1, RING) * 2 + core)
    sibling = (seq, x * 2 + 1 - core)
    ahead = (lax.rem(seq + 1, nseq), head)

    barrier = pltpu.get_barrier_semaphore()

    def greet(i, carry):
        pl.semaphore_signal(barrier, inc=1, device_id=(lax.rem(seq + i, nseq), head), device_id_type=MESH)
        return carry

    lax.fori_loop(1, nseq, greet, 0)
    for other in (right, left, sibling):
        pl.semaphore_signal(barrier, inc=1, device_id=other, device_id_type=MESH)

    loads = [
        pltpu.make_async_copy(src, dst, load_sem.at[i])
        for i, (src, dst) in enumerate(
            ((ld_hbm, ld), (k_hbm, k), (v_hbm, v), (q_hbm, q), (g_hbm, g), (gain_hbm, gain), (w_hbm, w))
        )
    ]
    for copy in loads:
        copy.start()

    fast = [trunc[h] < steps for h in range(2)]
    slow_f = [jnp.where(f, 0.0, 1.0).astype(F32) for f in fast]
    lower_i = lax.broadcasted_iota(jnp.int32, (BLOCK, BLOCK), 0)
    lower_j = lax.broadcasted_iota(jnp.int32, (BLOCK, BLOCK), 1)
    causal = lower_j <= lower_i
    tri = jnp.where(causal, 1.0, 0.0).astype(BF16)

    loads[0].wait()
    rates = ld[...].astype(F32)
    down, along, total = {}, {}, {}
    for h in range(2):
        for b in range(2):
            row = jnp.broadcast_to(rates[h : h + 1, b * BLOCK : (b + 1) * BLOCK], (128, BLOCK)).astype(BF16)
            down[h, b] = nt(tri, row)
            along[h, b] = nt(row[:16], tri)[:1]
            total[h, b] = down[h, b][BLOCK - 1 :]
            grow[h, b] = jnp.exp(down[h, b])

    loads[1].wait()
    loads[2].wait()
    for h in range(2):
        cols = pl.ds(h * DH, DH)
        own = []
        for b in range(2):
            rows = pl.ds(b * BLOCK, BLOCK)
            fade = twice(jnp.exp(total[h, b] - down[h, b]))
            own.append(tn((k[rows, cols].astype(F32) * fade).astype(BF16), v[rows, cols]))
        whole = own[0] * twice(jnp.exp(total[h, 1])) + own[1]
        state[pl.ds(h * 16, 16)] = whole.astype(BF16).reshape(16, 16, DH)
        first[h] = own[0]
        last[h] = own[1].astype(BF16)
        dec[h] = jnp.exp(total[h, 0] + total[h, 1]) * slow_f[h]

    pl.semaphore_wait(barrier, nseq + 2)

    def send_one(i, carry):
        t = lax.rem(seq + i, nseq)
        pltpu.make_async_remote_copy(
            state.at[t], pieces.at[seq], one_sem.at[0], one_sem.at[1], device_id=(t, head), device_id_type=MESH
        ).start()
        return carry

    lax.fori_loop(1, nseq, send_one, 0)

    def send_dec(i, carry):
        t = lax.rem(seq + i, nseq)
        pltpu.make_async_remote_copy(
            dec.at[lax.div(t, nseq // 2)], dec_in.at[seq], dec_sem.at[0], dec_sem.at[1],
            device_id=(t, head), device_id_type=MESH,
        ).start()
        return carry

    lax.fori_loop(1, nseq, send_dec, 0)
    pltpu.make_async_copy(state.at[seq], pieces.at[seq], one_sem.at[1]).start()
    pltpu.make_async_copy(dec.at[lax.div(seq, nseq // 2)], dec_in.at[seq], dec_sem.at[1]).start()
    last_copy = pltpu.make_async_remote_copy(
        last, last_in, last_sem.at[0], last_sem.at[1], device_id=ahead, device_id_type=MESH
    )
    last_copy.start()
    w_copy = pltpu.make_async_remote_copy(
        w_hbm, w_sib, wsib_sem.at[0], wsib_sem.at[1], device_id=sibling, device_id_type=MESH
    )
    w_copy.start()

    loads[3].wait()
    for h in range(2):
        cols = pl.ds(h * DH, DH)
        for b in range(2):
            rows = pl.ds(b * BLOCK, BLOCK)
            decay = jnp.exp(jnp.minimum(twice(down[h, b]) - along[h, b], 0.0))
            weights = jnp.where(causal, nt(q[rows, cols], k[rows, cols]) * decay, 0.0).astype(BF16)
            ret[rows, cols] = nn(weights, v[rows, cols])

    def wait_all(buffer, sem):
        pltpu.make_async_copy(buffer, buffer, sem).wait()

    def wait_sent(buffer, sem):
        most = buffer.at[pl.ds(0, nseq - 1)]
        pltpu.make_async_copy(most, most, sem).wait()

    wait_all(dec_in, dec_sem.at[1])
    wait_all(pieces, one_sem.at[1])

    def advance(n, total_state):
        prefixes[n] = total_state.astype(BF16)
        return total_state * twice(dec_in[n]) + pieces[n].astype(F32)

    lax.fori_loop(0, nseq, advance, jnp.zeros((16, DH), F32), unroll=4)

    def send_two(i, carry):
        t = lax.rem(seq + i, nseq)
        pltpu.make_async_remote_copy(
            prefixes.at[t], prior.at[seq], two_sem.at[0], two_sem.at[1], device_id=(t, head), device_id_type=MESH
        ).start()
        return carry

    lax.fori_loop(1, nseq, send_two, 0)
    pltpu.make_async_copy(prefixes.at[seq], prior.at[seq], two_sem.at[1]).start()

    loads[4].wait()
    loads[5].wait()
    gate = g[...].astype(F32)
    gated[...] = gain[...].astype(F32) * (gate / (1.0 + jnp.exp(-gate)))
    wait_sent(state, one_sem.at[0])
    wait_sent(dec_in, dec_sem.at[0])
    last_copy.wait()
    loads[6].wait()

    wait_all(prior, two_sem.at[1])
    started = jnp.where(seq > 0, 1.0, 0.0).astype(F32)
    before = {}
    for h in range(2):
        a = prior[pl.ds(h * 16, 16)].reshape(DH, DH)
        near_state = last_in[h].astype(F32) * ((1.0 - slow_f[h]) * started) + a.astype(F32) * slow_f[h]
        before[h, 0] = a
        before[h, 1] = (near_state * twice(jnp.exp(total[h, 0])) + first[h]).astype(BF16)
    for b in range(2):
        rows = pl.ds(b * BLOCK, BLOCK)
        for h in range(2):
            cols = pl.ds(h * DH, DH)
            kept = ret[rows, cols] + nn(q[rows, cols], before[h, b]) * twice(grow[h, b])
            mean = jnp.mean(kept, axis=1, keepdims=True)
            centered = kept - mean
            var = jnp.mean(centered * centered, axis=1, keepdims=True)
            hid[rows, cols] = (centered * lax.rsqrt(var + 1e-5) * gated[rows, cols]).astype(BF16)

    def rows_of(r, c):
        return pl.ds(pl.multiple_of((lax.rem(x + r, RING) * 2 + c) * PIECE, PIECE), PIECE)

    swaps = []
    for r in range(RING):
        copy = pltpu.make_async_remote_copy(
            hid.at[rows_of(r, 1 - core)], theirs.at[pl.ds(r * PIECE, PIECE)], hid_sem.at[0, r], hid_sem.at[1, r],
            device_id=sibling, device_id_type=MESH,
        )
        copy.start()
        swaps.append(copy)
    for r in range(RING):
        mine[pl.ds(r * PIECE, PIECE)] = hid[rows_of(r, core)]
    w_copy.wait_recv()
    for copy in swaps:
        copy.wait_recv()

    def push(kind, j, side, src, dst, to):
        return pltpu.make_async_remote_copy(
            src, dst, p_send.at[kind, j, side], p_recv.at[kind, j, side], device_id=to, device_id_type=MESH
        )

    def far(j, side):
        return push(0, j, side, part.at[j, 2, side], passed.at[j, side], (left, right)[side])

    def near(j, side):
        return push(1, j, side, part.at[j, (1, 3)[side], side], direct.at[j, side], (right, left)[side])

    def onward(j, side):
        return push(2, j, side, part.at[j, (3, 1)[side], side], summed.at[j, side], (left, right)[side])

    def project(j, carry):
        cols = pl.ds(pl.multiple_of(j * CHUNK, CHUNK), CHUNK)
        product = (nn(mine[...], w[:, cols]) + nn(theirs[...], w_sib[:, cols])).astype(BF16)
        for r in range(RING):
            for side in range(2):
                part[j, r, side] = product[r * PIECE : (r + 1) * PIECE, side * HALF : (side + 1) * HALF]
        far(j, 0).start()
        far(j, 1).start()
        near(j, 0).start()
        near(j, 1).start()
        return carry

    lax.fori_loop(0, nchunk, project, 0)

    def forward(j, carry):
        for side in range(2):
            far(j, side).wait_recv()
            slot = (3, 1)[side]
            part[j, slot, side] = (part[j, slot, side].astype(F32) + passed[j, side].astype(F32)).astype(BF16)
            onward(j, side).start()
        return carry

    lax.fori_loop(0, nchunk, forward, 0)

    def write(j):
        cols = pl.ds(pl.multiple_of(j * CHUNK, CHUNK), CHUNK)
        return pltpu.make_async_copy(out.at[:, cols], out_hbm.at[:, cols], out_sem.at[j])

    def finish(j, carry):
        for side in range(2):
            near(j, side).wait_recv()
            onward(j, side).wait_recv()
            cols = pl.ds(pl.multiple_of(j * CHUNK + side * HALF, HALF), HALF)
            out[:, cols] = (
                part[j, 0, side].astype(F32) + direct[j, side].astype(F32) + summed[j, side].astype(F32)
            ).astype(BF16)
        write(j).start()
        return carry

    lax.fori_loop(0, nchunk, finish, 0)

    def drain(j, carry):
        for side in range(2):
            far(j, side).wait_send()
            near(j, side).wait_send()
            onward(j, side).wait_send()
        write(j).wait()
        return carry

    lax.fori_loop(0, nchunk, drain, 0)
    w_copy.wait_send()
    for copy in swaps:
        copy.wait_send()
    wait_sent(prefixes, two_sem.at[0])


def on_device(queries, keys, values, gate, log_decay, trunc_blocks, norm_gain, w_out):
    nseq = lax.axis_size("seq")
    tokens, width = queries.shape
    columns = w_out.shape[1]
    nchunk = columns // CHUNK
    any_spec = pl.BlockSpec(memory_space=pl.ANY)
    vmem, dma = pltpu.VMEM, pltpu.SemaphoreType.DMA
    return pl.pallas_call(
        functools.partial(kernel, nseq, nchunk, tokens // BLOCK * nseq),
        out_shape=jax.ShapeDtypeStruct((PIECE, columns), BF16),
        in_specs=[any_spec] * 5 + [pl.BlockSpec(memory_space=pltpu.SMEM)] + [any_spec] * 2,
        out_specs=any_spec,
        scratch_shapes=[
            vmem((tokens, width), BF16),
            vmem((tokens, width), BF16),
            vmem((tokens, width), BF16),
            vmem((tokens, width), BF16),
            vmem((2, tokens), BF16),
            vmem((1, width), BF16),
            vmem((width, columns), BF16),
            vmem((width, columns), BF16),
            vmem((nseq, 16, DH), BF16),
            vmem((2, DH, DH), F32),
            vmem((2, DH, DH), BF16),
            vmem((2, DH, DH), BF16),
            vmem((2, 1, 128), F32),
            vmem((nseq, 1, 128), F32),
            vmem((nseq, 16, DH), BF16),
            vmem((nseq, 16, DH), BF16),
            vmem((nseq, 16, DH), BF16),
            vmem((tokens, width), F32),
            vmem((tokens, width), F32),
            vmem((2, 2, BLOCK, 128), F32),
            vmem((tokens, width), BF16),
            vmem((RING * PIECE, width), BF16),
            vmem((RING * PIECE, width), BF16),
            vmem((nchunk, RING, 2, PIECE, HALF), BF16),
            vmem((nchunk, 2, PIECE, HALF), BF16),
            vmem((nchunk, 2, PIECE, HALF), BF16),
            vmem((nchunk, 2, PIECE, HALF), BF16),
            vmem((PIECE, columns), BF16),
            dma((7,)),
            dma((2,)),
            dma((2,)),
            dma((2,)),
            dma((2,)),
            dma((2,)),
            dma((2, RING)),
            dma((3, nchunk, 2)),
            dma((3, nchunk, 2)),
            dma((nchunk,)),
        ],
        compiler_params=pltpu.CompilerParams(
            collective_id=0, has_side_effects=True, vmem_limit_bytes=56 * 2**20
        ),
        cost_estimate=pl.CostEstimate(flops=3 * 10**9, bytes_accessed=7 * 2**20, transcendentals=2**20),
    )(queries, keys, values, gate, log_decay, trunc_blocks, norm_gain.reshape(1, width), w_out)


def solution(mesh):
    in_specs = (
        P("seq", "head"),
        P("seq", "head"),
        P("seq", "head"),
        P("seq", "head"),
        P("head", "seq"),
        P("head"),
        P("head"),
        P("head", None),
    )
    out_specs = P(("seq", "head"), None)
    return jax.shard_map(on_device, mesh=mesh, in_specs=in_specs, out_specs=out_specs, check_vma=False)
```

```python
import functools

import jax
import jax.numpy as jnp
from jax import lax
from jax.experimental import pallas as pl
from jax.experimental.pallas import tpu as pltpu
from jax.sharding import PartitionSpec as P

MESH = pl.DeviceIdType.MESH
F32 = jnp.float32
BF16 = jnp.bfloat16
BLOCK = 256
DH = 256
CHUNK = 512
HALF = CHUNK // 2
PIECE = 64
RING = 4
GROUP = 8
SHARE = 2 * DH // GROUP


def nt(a, b):
    return lax.dot_general(a, b, (((1,), (1,)), ((), ())), preferred_element_type=F32)


def tn(a, b):
    return lax.dot_general(a, b, (((0,), (0,)), ((), ())), preferred_element_type=F32)


def nn(a, b):
    return jnp.dot(a, b, preferred_element_type=F32)


def twice(a):
    return jnp.concatenate([a, a], axis=1)


def kernel(
    nseq, nchunk, steps,
    q_hbm, k_hbm, v_hbm, g_hbm, ld_hbm, trunc, gain_hbm, w_hbm,
    out_hbm,
    q, k, v, g, ld, gain, w, w_sib,
    state, first, last, last_in, dec, dec_in, pieces, prefixes, prior, sums, sums_in, fades, fades_in,
    ret, gated, grow, hid, mine, theirs, part, passed, direct, summed, out,
    load_sem, dec_sem, one_sem, two_sem, last_sem, sum_send, sum_recv, fade_send, fade_recv, ready, ready_last,
    wsib_sem, hid_sem, p_send, p_recv, out_sem,
):
    seq, head = lax.axis_index("seq"), lax.axis_index("head")
    x, core = lax.div(head, 2), lax.rem(head, 2)
    right = (seq, lax.rem(x + 1, RING) * 2 + core)
    left = (seq, lax.rem(x + RING - 1, RING) * 2 + core)
    sibling = (seq, x * 2 + 1 - core)
    group, place = lax.div(seq, GROUP), lax.rem(seq, GROUP)
    groups = nseq // GROUP
    inside = place < GROUP - 1
    crossing = jnp.logical_and(place == GROUP - 1, group < groups - 1)
    crossed = jnp.logical_and(place == 0, group > 0)

    def fellow(i):
        return group * GROUP + lax.rem(place + i, GROUP)

    def abreast(other):
        return (other * GROUP + place, head)

    barrier = pltpu.get_barrier_semaphore()

    def greet(i, carry):
        pl.semaphore_signal(barrier, inc=1, device_id=(fellow(i), head), device_id_type=MESH)
        return carry

    def greet_later(other, carry):
        pl.semaphore_signal(barrier, inc=1, device_id=abreast(other), device_id_type=MESH)
        return carry

    lax.fori_loop(1, GROUP, greet, 0)
    lax.fori_loop(group + 1, groups, greet_later, 0)

    @pl.when(crossing)
    def _():
        pl.semaphore_signal(barrier, inc=1, device_id=(seq + 1, head), device_id_type=MESH)

    for other in (right, left, sibling):
        pl.semaphore_signal(barrier, inc=1, device_id=other, device_id_type=MESH)

    loads = [
        pltpu.make_async_copy(src, dst, load_sem.at[i])
        for i, (src, dst) in enumerate(
            ((ld_hbm, ld), (k_hbm, k), (v_hbm, v), (q_hbm, q), (g_hbm, g), (gain_hbm, gain), (w_hbm, w))
        )
    ]
    for copy in loads:
        copy.start()

    fast = [trunc[h] < steps for h in range(2)]
    slow_f = [jnp.where(f, 0.0, 1.0).astype(F32) for f in fast]
    lower_i = lax.broadcasted_iota(jnp.int32, (BLOCK, BLOCK), 0)
    lower_j = lax.broadcasted_iota(jnp.int32, (BLOCK, BLOCK), 1)
    causal = lower_j <= lower_i
    tri = jnp.where(causal, 1.0, 0.0).astype(BF16)

    loads[0].wait()
    rates = ld[...].astype(F32)
    down, along, total = {}, {}, {}
    for h in range(2):
        for b in range(2):
            row = jnp.broadcast_to(rates[h : h + 1, b * BLOCK : (b + 1) * BLOCK], (128, BLOCK)).astype(BF16)
            down[h, b] = nt(tri, row)
            along[h, b] = nt(row[:16], tri)[:1]
            total[h, b] = down[h, b][BLOCK - 1 :]
            grow[h, b] = jnp.exp(down[h, b])

    loads[1].wait()
    loads[2].wait()
    for h in range(2):
        cols = pl.ds(h * DH, DH)
        own = []
        for b in range(2):
            rows = pl.ds(b * BLOCK, BLOCK)
            fade = twice(jnp.exp(total[h, b] - down[h, b]))
            own.append(tn((k[rows, cols].astype(F32) * fade).astype(BF16), v[rows, cols]))
        whole = own[0] * twice(jnp.exp(total[h, 1])) + own[1]
        state[pl.ds(h * (GROUP // 2), GROUP // 2)] = whole.astype(BF16).reshape(GROUP // 2, SHARE, DH)
        first[h] = own[0]
        last[h] = own[1].astype(BF16)
        dec[h] = jnp.exp(total[h, 0] + total[h, 1]) * slow_f[h]

    pl.semaphore_wait(barrier, GROUP + 2 + group + jnp.where(crossed, 1, 0))

    def tell(other, carry):
        pl.semaphore_signal(ready.at[group], inc=1, device_id=abreast(other), device_id_type=MESH)
        return carry

    lax.fori_loop(0, group, tell, 0)

    @pl.when(crossed)
    def _():
        pl.semaphore_signal(ready_last, inc=1, device_id=(seq - 1, head), device_id_type=MESH)

    def send_one(i, carry):
        t = lax.rem(place + i, GROUP)
        pltpu.make_async_remote_copy(
            state.at[t], pieces.at[place], one_sem.at[0], one_sem.at[1],
            device_id=(fellow(i), head), device_id_type=MESH,
        ).start()
        return carry

    lax.fori_loop(1, GROUP, send_one, 0)

    def send_dec(i, carry):
        t = lax.rem(place + i, GROUP)
        pltpu.make_async_remote_copy(
            dec.at[lax.div(t, GROUP // 2)], dec_in.at[place], dec_sem.at[0], dec_sem.at[1],
            device_id=(fellow(i), head), device_id_type=MESH,
        ).start()
        return carry

    lax.fori_loop(1, GROUP, send_dec, 0)
    pltpu.make_async_copy(state.at[place], pieces.at[place], one_sem.at[1]).start()
    pltpu.make_async_copy(dec.at[lax.div(place, GROUP // 2)], dec_in.at[place], dec_sem.at[1]).start()

    last_copy = pltpu.make_async_remote_copy(
        last, last_in, last_sem.at[0], last_sem.at[1], device_id=(lax.rem(seq + 1, nseq), head), device_id_type=MESH
    )

    @pl.when(inside)
    def _():
        last_copy.start()

    w_copy = pltpu.make_async_remote_copy(
        w_hbm, w_sib, wsib_sem.at[0], wsib_sem.at[1], device_id=sibling, device_id_type=MESH
    )
    w_copy.start()

    loads[3].wait()
    for h in range(2):
        cols = pl.ds(h * DH, DH)
        for b in range(2):
            rows = pl.ds(b * BLOCK, BLOCK)
            decay = jnp.exp(jnp.minimum(twice(down[h, b]) - along[h, b], 0.0))
            weights = jnp.where(causal, nt(q[rows, cols], k[rows, cols]) * decay, 0.0).astype(BF16)
            ret[rows, cols] = nn(weights, v[rows, cols])

    @pl.when(crossing)
    def _():
        pl.semaphore_wait(ready_last, 1)
        last_copy.start()

    def wait_all(buffer, sem):
        pltpu.make_async_copy(buffer, buffer, sem).wait()

    def wait_sent(buffer, sem):
        most = buffer.at[pl.ds(0, GROUP - 1)]
        pltpu.make_async_copy(most, most, sem).wait()

    wait_all(dec_in, dec_sem.at[1])
    wait_all(pieces, one_sem.at[1])

    so_far, fade_so_far = jnp.zeros((SHARE, DH), F32), jnp.ones((1, 128), F32)
    for n in range(GROUP):
        so_far = so_far * twice(dec_in[n]) + pieces[n].astype(F32)
        fade_so_far = fade_so_far * dec_in[n]
    sums[...] = so_far.astype(BF16)
    fades[...] = fade_so_far

    def sum_copy(source, target):
        return pltpu.make_async_remote_copy(
            sums, sums_in.at[source], sum_send.at[target], sum_recv.at[source],
            device_id=abreast(target), device_id_type=MESH,
        )

    def fade_copy(source, target):
        return pltpu.make_async_remote_copy(
            fades, fades_in.at[source], fade_send.at[target], fade_recv.at[source],
            device_id=abreast(target), device_id_type=MESH,
        )

    def send_sum(other, carry):
        pl.semaphore_wait(ready.at[other], 1)
        sum_copy(group, other).start()
        fade_copy(group, other).start()
        return carry

    lax.fori_loop(group + 1, groups, send_sum, 0)

    def add_group(other, total_state):
        fade_copy(other, group).wait_recv()
        sum_copy(other, group).wait_recv()
        return total_state * twice(fades_in[other]) + sums_in[other].astype(F32)

    total_state = lax.fori_loop(0, group, add_group, jnp.zeros((SHARE, DH), F32))

    for n in range(GROUP):
        prefixes[n] = total_state.astype(BF16)
        total_state = total_state * twice(dec_in[n]) + pieces[n].astype(F32)

    def send_two(i, carry):
        t = lax.rem(place + i, GROUP)
        pltpu.make_async_remote_copy(
            prefixes.at[t], prior.at[place], two_sem.at[0], two_sem.at[1],
            device_id=(fellow(i), head), device_id_type=MESH,
        ).start()
        return carry

    lax.fori_loop(1, GROUP, send_two, 0)
    pltpu.make_async_copy(prefixes.at[place], prior.at[place], two_sem.at[1]).start()

    loads[4].wait()
    loads[5].wait()
    gate, width = g[...].astype(F32), g.shape[1]
    gated[...] = gain[...].astype(F32).reshape(1, width) * (gate / (1.0 + jnp.exp(-gate)))
    wait_sent(state, one_sem.at[0])
    wait_sent(dec_in, dec_sem.at[0])

    @pl.when(jnp.logical_or(inside, crossing))
    def _():
        last_copy.wait_send()

    def sums_sent(other, carry):
        sum_copy(group, other).wait_send()
        fade_copy(group, other).wait_send()
        return carry

    lax.fori_loop(group + 1, groups, sums_sent, 0)
    loads[6].wait()

    @pl.when(seq > 0)
    def _():
        last_copy.wait_recv()

    @pl.when(seq == 0)
    def _():
        last_in[...] = jnp.zeros_like(last_in)


    wait_all(prior, two_sem.at[1])
    before = {}
    for h in range(2):
        a = prior[pl.ds(h * (GROUP // 2), GROUP // 2)].reshape(DH, DH)
        near_state = last_in[h].astype(F32) * (1.0 - slow_f[h]) + a.astype(F32) * slow_f[h]
        before[h, 0] = a
        before[h, 1] = (near_state * twice(jnp.exp(total[h, 0])) + first[h]).astype(BF16)
    for b in range(2):
        rows = pl.ds(b * BLOCK, BLOCK)
        for h in range(2):
            cols = pl.ds(h * DH, DH)
            kept = ret[rows, cols] + nn(q[rows, cols], before[h, b]) * twice(grow[h, b])
            mean = jnp.mean(kept, axis=1, keepdims=True)
            centered = kept - mean
            var = jnp.mean(centered * centered, axis=1, keepdims=True)
            hid[rows, cols] = (centered * lax.rsqrt(var + 1e-5) * gated[rows, cols]).astype(BF16)

    def rows_of(r, c):
        return pl.ds(pl.multiple_of((lax.rem(x + r, RING) * 2 + c) * PIECE, PIECE), PIECE)

    swaps = []
    for r in range(RING):
        copy = pltpu.make_async_remote_copy(
            hid.at[rows_of(r, 1 - core)], theirs.at[pl.ds(r * PIECE, PIECE)], hid_sem.at[0, r], hid_sem.at[1, r],
            device_id=sibling, device_id_type=MESH,
        )
        copy.start()
        swaps.append(copy)
    for r in range(RING):
        mine[pl.ds(r * PIECE, PIECE)] = hid[rows_of(r, core)]
    w_copy.wait_recv()
    for copy in swaps:
        copy.wait_recv()

    def push(kind, j, side, src, dst, to):
        return pltpu.make_async_remote_copy(
            src, dst, p_send.at[kind, j, side], p_recv.at[kind, j, side], device_id=to, device_id_type=MESH
        )

    def far(j, side):
        return push(0, j, side, part.at[j, 2, side], passed.at[j, side], (left, right)[side])

    def near(j, side):
        return push(1, j, side, part.at[j, (1, 3)[side], side], direct.at[j, side], (right, left)[side])

    def onward(j, side):
        return push(2, j, side, part.at[j, (3, 1)[side], side], summed.at[j, side], (left, right)[side])

    def project(j, carry):
        cols = pl.ds(pl.multiple_of(j * CHUNK, CHUNK), CHUNK)
        product = (nn(mine[...], w[:, cols]) + nn(theirs[...], w_sib[:, cols])).astype(BF16)
        for r in range(RING):
            for side in range(2):
                part[j, r, side] = product[r * PIECE : (r + 1) * PIECE, side * HALF : (side + 1) * HALF]
        far(j, 0).start()
        far(j, 1).start()
        near(j, 0).start()
        near(j, 1).start()
        return carry

    lax.fori_loop(0, nchunk, project, 0)

    def forward(j, carry):
        for side in range(2):
            far(j, side).wait_recv()
            slot = (3, 1)[side]
            part[j, slot, side] = (part[j, slot, side].astype(F32) + passed[j, side].astype(F32)).astype(BF16)
            onward(j, side).start()
        return carry

    lax.fori_loop(0, nchunk, forward, 0)

    def write(j):
        cols = pl.ds(pl.multiple_of(j * CHUNK, CHUNK), CHUNK)
        return pltpu.make_async_copy(out.at[:, cols], out_hbm.at[:, cols], out_sem.at[j])

    def finish(j, carry):
        for side in range(2):
            near(j, side).wait_recv()
            onward(j, side).wait_recv()
            cols = pl.ds(pl.multiple_of(j * CHUNK + side * HALF, HALF), HALF)
            out[:, cols] = (
                part[j, 0, side].astype(F32) + direct[j, side].astype(F32) + summed[j, side].astype(F32)
            ).astype(BF16)
        write(j).start()
        return carry

    lax.fori_loop(0, nchunk, finish, 0)

    def drain(j, carry):
        for side in range(2):
            far(j, side).wait_send()
            near(j, side).wait_send()
            onward(j, side).wait_send()
        write(j).wait()
        return carry

    lax.fori_loop(0, nchunk, drain, 0)
    w_copy.wait_send()
    for copy in swaps:
        copy.wait_send()
    wait_sent(prefixes, two_sem.at[0])


def on_device(queries, keys, values, gate, log_decay, trunc_blocks, norm_gain, w_out):
    nseq = lax.axis_size("seq")
    tokens, width = queries.shape
    columns = w_out.shape[1]
    nchunk, groups = columns // CHUNK, nseq // GROUP
    any_spec = pl.BlockSpec(memory_space=pl.ANY)
    vmem, dma = pltpu.VMEM, pltpu.SemaphoreType.DMA
    return pl.pallas_call(
        functools.partial(kernel, nseq, nchunk, tokens // BLOCK * nseq),
        out_shape=jax.ShapeDtypeStruct((PIECE, columns), BF16),
        in_specs=[any_spec] * 5 + [pl.BlockSpec(memory_space=pltpu.SMEM)] + [any_spec] * 2,
        out_specs=any_spec,
        scratch_shapes=[
            vmem((tokens, width), BF16),
            vmem((tokens, width), BF16),
            vmem((tokens, width), BF16),
            vmem((tokens, width), BF16),
            vmem((2, tokens), BF16),
            vmem((width,), BF16),
            vmem((width, columns), BF16),
            vmem((width, columns), BF16),
            vmem((GROUP, SHARE, DH), BF16),
            vmem((2, DH, DH), F32),
            vmem((2, DH, DH), BF16),
            vmem((2, DH, DH), BF16),
            vmem((2, 1, 128), F32),
            vmem((GROUP, 1, 128), F32),
            vmem((GROUP, SHARE, DH), BF16),
            vmem((GROUP, SHARE, DH), BF16),
            vmem((GROUP, SHARE, DH), BF16),
            vmem((SHARE, DH), BF16),
            vmem((groups, SHARE, DH), BF16),
            vmem((1, 128), F32),
            vmem((groups, 1, 128), F32),
            vmem((tokens, width), F32),
            vmem((tokens, width), F32),
            vmem((2, 2, BLOCK, 128), F32),
            vmem((tokens, width), BF16),
            vmem((RING * PIECE, width), BF16),
            vmem((RING * PIECE, width), BF16),
            vmem((nchunk, RING, 2, PIECE, HALF), BF16),
            vmem((nchunk, 2, PIECE, HALF), BF16),
            vmem((nchunk, 2, PIECE, HALF), BF16),
            vmem((nchunk, 2, PIECE, HALF), BF16),
            vmem((PIECE, columns), BF16),
            dma((7,)),
            dma((2,)),
            dma((2,)),
            dma((2,)),
            dma((2,)),
            dma((groups,)),
            dma((groups,)),
            dma((groups,)),
            dma((groups,)),
            pltpu.SemaphoreType.REGULAR((groups,)),
            pltpu.SemaphoreType.REGULAR,
            dma((2,)),
            dma((2, RING)),
            dma((3, nchunk, 2)),
            dma((3, nchunk, 2)),
            dma((nchunk,)),
        ],
        compiler_params=pltpu.CompilerParams(
            collective_id=0, has_side_effects=True, vmem_limit_bytes=56 * 2**20
        ),
        cost_estimate=pl.CostEstimate(flops=3 * 10**9, bytes_accessed=7 * 2**20, transcendentals=2**20),
    )(queries, keys, values, gate, log_decay, trunc_blocks, norm_gain, w_out)


def solution(mesh):
    in_specs = (
        P("seq", "head"),
        P("seq", "head"),
        P("seq", "head"),
        P("seq", "head"),
        P("head", "seq"),
        P("head"),
        P("head"),
        P("head", None),
    )
    out_specs = P(("seq", "head"), None)
    return jax.shard_map(on_device, mesh=mesh, in_specs=in_specs, out_specs=out_specs, check_vma=False)
```

```python
import functools

import jax
import jax.numpy as jnp
from jax import lax
from jax.experimental import pallas as pl
from jax.experimental.pallas import tpu as pltpu
from jax.sharding import PartitionSpec as P

MESH = pl.DeviceIdType.MESH
F32 = jnp.float32
BF16 = jnp.bfloat16
BLOCK = 256
DH = 256
CHUNK = 512
HALF = CHUNK // 2
PIECE = 64
RING = 4
GROUP = 8
SHARE = 2 * DH // GROUP


def nt(a, b):
    return lax.dot_general(a, b, (((1,), (1,)), ((), ())), preferred_element_type=F32)


def tn(a, b):
    return lax.dot_general(a, b, (((0,), (0,)), ((), ())), preferred_element_type=F32)


def nn(a, b):
    return jnp.dot(a, b, preferred_element_type=F32)


def twice(a):
    return jnp.concatenate([a, a], axis=1)


def kernel(
    nseq, nchunk, steps,
    q_hbm, k_hbm, v_hbm, g_hbm, ld_hbm, trunc, gain_hbm, w_hbm,
    out,
    q, k, v, g, ld, gain, w, w_sib,
    state, first, last, last_in, dec, dec_in, pieces, prefixes, prior, sums, sums_in, fades, fades_in,
    ret, gated, grow, hid, mine, theirs, part, passed, direct, summed,
    load_sem, dec_sem, one_sem, two_sem, last_sem, sum_send, sum_recv, fade_send, fade_recv, ready, ready_last,
    wsib_sem, hid_sem, p_send, p_recv,
):
    seq, head = lax.axis_index("seq"), lax.axis_index("head")
    x, core = lax.div(head, 2), lax.rem(head, 2)
    right = (seq, lax.rem(x + 1, RING) * 2 + core)
    left = (seq, lax.rem(x + RING - 1, RING) * 2 + core)
    sibling = (seq, x * 2 + 1 - core)
    group, place = lax.div(seq, GROUP), lax.rem(seq, GROUP)
    groups = nseq // GROUP
    inside = place < GROUP - 1
    crossing = jnp.logical_and(place == GROUP - 1, group < groups - 1)
    crossed = jnp.logical_and(place == 0, group > 0)

    def fellow(i):
        return group * GROUP + lax.rem(place + i, GROUP)

    def abreast(other):
        return (other * GROUP + place, head)

    barrier = pltpu.get_barrier_semaphore()

    def greet(i, carry):
        pl.semaphore_signal(barrier, inc=1, device_id=(fellow(i), head), device_id_type=MESH)
        return carry

    def greet_later(other, carry):
        pl.semaphore_signal(barrier, inc=1, device_id=abreast(other), device_id_type=MESH)
        return carry

    lax.fori_loop(1, GROUP, greet, 0)
    lax.fori_loop(group + 1, groups, greet_later, 0)

    @pl.when(crossing)
    def _():
        pl.semaphore_signal(barrier, inc=1, device_id=(seq + 1, head), device_id_type=MESH)

    for other in (right, left, sibling):
        pl.semaphore_signal(barrier, inc=1, device_id=other, device_id_type=MESH)

    loads = [
        pltpu.make_async_copy(src, dst, load_sem.at[i])
        for i, (src, dst) in enumerate(
            ((ld_hbm, ld), (k_hbm, k), (v_hbm, v), (q_hbm, q), (g_hbm, g), (gain_hbm, gain), (w_hbm, w))
        )
    ]
    for copy in loads:
        copy.start()

    fast = [trunc[h] < steps for h in range(2)]
    slow_f = [jnp.where(f, 0.0, 1.0).astype(F32) for f in fast]
    lower_i = lax.broadcasted_iota(jnp.int32, (BLOCK, BLOCK), 0)
    lower_j = lax.broadcasted_iota(jnp.int32, (BLOCK, BLOCK), 1)
    causal = lower_j <= lower_i
    tri = jnp.where(causal, 1.0, 0.0).astype(BF16)

    loads[0].wait()
    rates = ld[...].astype(F32)
    down, along, total = {}, {}, {}
    for h in range(2):
        for b in range(2):
            row = jnp.broadcast_to(rates[h : h + 1, b * BLOCK : (b + 1) * BLOCK], (128, BLOCK)).astype(BF16)
            down[h, b] = nt(tri, row)
            along[h, b] = nt(row[:16], tri)[:1]
            total[h, b] = down[h, b][BLOCK - 1 :]
            grow[h, b] = jnp.exp(down[h, b])

    loads[1].wait()
    loads[2].wait()
    for h in range(2):
        cols = pl.ds(h * DH, DH)
        own = []
        for b in range(2):
            rows = pl.ds(b * BLOCK, BLOCK)
            fade = twice(jnp.exp(total[h, b] - down[h, b]))
            own.append(tn((k[rows, cols].astype(F32) * fade).astype(BF16), v[rows, cols]))
        whole = own[0] * twice(jnp.exp(total[h, 1])) + own[1]
        state[pl.ds(h * (GROUP // 2), GROUP // 2)] = whole.astype(BF16).reshape(GROUP // 2, SHARE, DH)
        first[h] = own[0]
        last[h] = own[1].astype(BF16)
        dec[h] = jnp.exp(total[h, 0] + total[h, 1]) * slow_f[h]

    pl.semaphore_wait(barrier, GROUP + 2 + group + jnp.where(crossed, 1, 0))

    def tell(other, carry):
        pl.semaphore_signal(ready.at[group], inc=1, device_id=abreast(other), device_id_type=MESH)
        return carry

    lax.fori_loop(0, group, tell, 0)

    @pl.when(crossed)
    def _():
        pl.semaphore_signal(ready_last, inc=1, device_id=(seq - 1, head), device_id_type=MESH)

    def send_one(i, carry):
        t = lax.rem(place + i, GROUP)
        pltpu.make_async_remote_copy(
            state.at[t], pieces.at[place], one_sem.at[0], one_sem.at[1],
            device_id=(fellow(i), head), device_id_type=MESH,
        ).start()
        return carry

    lax.fori_loop(1, GROUP, send_one, 0)

    def send_dec(i, carry):
        t = lax.rem(place + i, GROUP)
        pltpu.make_async_remote_copy(
            dec.at[lax.div(t, GROUP // 2)], dec_in.at[place], dec_sem.at[0], dec_sem.at[1],
            device_id=(fellow(i), head), device_id_type=MESH,
        ).start()
        return carry

    lax.fori_loop(1, GROUP, send_dec, 0)
    pltpu.make_async_copy(state.at[place], pieces.at[place], one_sem.at[1]).start()
    pltpu.make_async_copy(dec.at[lax.div(place, GROUP // 2)], dec_in.at[place], dec_sem.at[1]).start()

    last_copy = pltpu.make_async_remote_copy(
        last, last_in, last_sem.at[0], last_sem.at[1], device_id=(lax.rem(seq + 1, nseq), head), device_id_type=MESH
    )

    @pl.when(inside)
    def _():
        last_copy.start()

    w_copy = pltpu.make_async_remote_copy(
        w_hbm, w_sib, wsib_sem.at[0], wsib_sem.at[1], device_id=sibling, device_id_type=MESH
    )
    w_copy.start()

    loads[3].wait()
    for h in range(2):
        cols = pl.ds(h * DH, DH)
        for b in range(2):
            rows = pl.ds(b * BLOCK, BLOCK)
            decay = jnp.exp(jnp.minimum(twice(down[h, b]) - along[h, b], 0.0))
            weights = jnp.where(causal, nt(q[rows, cols], k[rows, cols]) * decay, 0.0).astype(BF16)
            ret[rows, cols] = nn(weights, v[rows, cols])

    @pl.when(crossing)
    def _():
        pl.semaphore_wait(ready_last, 1)
        last_copy.start()

    def wait_all(buffer, sem):
        pltpu.make_async_copy(buffer, buffer, sem).wait()

    def wait_sent(buffer, sem):
        most = buffer.at[pl.ds(0, GROUP - 1)]
        pltpu.make_async_copy(most, most, sem).wait()

    wait_all(dec_in, dec_sem.at[1])
    wait_all(pieces, one_sem.at[1])

    so_far, fade_so_far = jnp.zeros((SHARE, DH), F32), jnp.ones((1, 128), F32)
    for n in range(GROUP):
        so_far = so_far * twice(dec_in[n]) + pieces[n].astype(F32)
        fade_so_far = fade_so_far * dec_in[n]
    sums[...] = so_far.astype(BF16)
    fades[...] = fade_so_far

    def sum_copy(source, target):
        return pltpu.make_async_remote_copy(
            sums, sums_in.at[source], sum_send.at[target], sum_recv.at[source],
            device_id=abreast(target), device_id_type=MESH,
        )

    def fade_copy(source, target):
        return pltpu.make_async_remote_copy(
            fades, fades_in.at[source], fade_send.at[target], fade_recv.at[source],
            device_id=abreast(target), device_id_type=MESH,
        )

    def send_sum(other, carry):
        pl.semaphore_wait(ready.at[other], 1)
        sum_copy(group, other).start()
        fade_copy(group, other).start()
        return carry

    lax.fori_loop(group + 1, groups, send_sum, 0)

    def add_group(other, total_state):
        fade_copy(other, group).wait_recv()
        sum_copy(other, group).wait_recv()
        return total_state * twice(fades_in[other]) + sums_in[other].astype(F32)

    total_state = lax.fori_loop(0, group, add_group, jnp.zeros((SHARE, DH), F32))

    for n in range(GROUP):
        prefixes[n] = total_state.astype(BF16)
        total_state = total_state * twice(dec_in[n]) + pieces[n].astype(F32)

    def send_two(i, carry):
        t = lax.rem(place + i, GROUP)
        pltpu.make_async_remote_copy(
            prefixes.at[t], prior.at[place], two_sem.at[0], two_sem.at[1],
            device_id=(fellow(i), head), device_id_type=MESH,
        ).start()
        return carry

    lax.fori_loop(1, GROUP, send_two, 0)
    pltpu.make_async_copy(prefixes.at[place], prior.at[place], two_sem.at[1]).start()

    loads[4].wait()
    loads[5].wait()
    gate, width = g[...].astype(F32), g.shape[1]
    gated[...] = gain[...].astype(F32).reshape(1, width) * (gate / (1.0 + jnp.exp(-gate)))
    wait_sent(state, one_sem.at[0])
    wait_sent(dec_in, dec_sem.at[0])

    @pl.when(jnp.logical_or(inside, crossing))
    def _():
        last_copy.wait_send()

    def sums_sent(other, carry):
        sum_copy(group, other).wait_send()
        fade_copy(group, other).wait_send()
        return carry

    lax.fori_loop(group + 1, groups, sums_sent, 0)
    loads[6].wait()

    @pl.when(seq > 0)
    def _():
        last_copy.wait_recv()

    @pl.when(seq == 0)
    def _():
        last_in[...] = jnp.zeros_like(last_in)


    wait_all(prior, two_sem.at[1])
    before = {}
    for h in range(2):
        a = prior[pl.ds(h * (GROUP // 2), GROUP // 2)].reshape(DH, DH)
        near_state = last_in[h].astype(F32) * (1.0 - slow_f[h]) + a.astype(F32) * slow_f[h]
        before[h, 0] = a
        before[h, 1] = (near_state * twice(jnp.exp(total[h, 0])) + first[h]).astype(BF16)
    for b in range(2):
        rows = pl.ds(b * BLOCK, BLOCK)
        for h in range(2):
            cols = pl.ds(h * DH, DH)
            kept = ret[rows, cols] + nn(q[rows, cols], before[h, b]) * twice(grow[h, b])
            mean = jnp.mean(kept, axis=1, keepdims=True)
            centered = kept - mean
            var = jnp.mean(centered * centered, axis=1, keepdims=True)
            hid[rows, cols] = (centered * lax.rsqrt(var + 1e-5) * gated[rows, cols]).astype(BF16)

    def rows_of(r, c):
        return pl.ds(pl.multiple_of((lax.rem(x + r, RING) * 2 + c) * PIECE, PIECE), PIECE)

    swaps = []
    for r in range(RING):
        copy = pltpu.make_async_remote_copy(
            hid.at[rows_of(r, 1 - core)], theirs.at[pl.ds(r * PIECE, PIECE)], hid_sem.at[0, r], hid_sem.at[1, r],
            device_id=sibling, device_id_type=MESH,
        )
        copy.start()
        swaps.append(copy)
    for r in range(RING):
        mine[pl.ds(r * PIECE, PIECE)] = hid[rows_of(r, core)]
    w_copy.wait_recv()
    for copy in swaps:
        copy.wait_recv()

    def push(kind, j, side, src, dst, to):
        return pltpu.make_async_remote_copy(
            src, dst, p_send.at[kind, j, side], p_recv.at[kind, j, side], device_id=to, device_id_type=MESH
        )

    def far(j, side):
        return push(0, j, side, part.at[j, 2, side], passed.at[j, side], (left, right)[side])

    def near(j, side):
        return push(1, j, side, part.at[j, (1, 3)[side], side], direct.at[j, side], (right, left)[side])

    def onward(j, side):
        return push(2, j, side, part.at[j, (3, 1)[side], side], summed.at[j, side], (left, right)[side])

    def project(j, carry):
        cols = pl.ds(pl.multiple_of(j * CHUNK, CHUNK), CHUNK)
        product = (nn(mine[...], w[:, cols]) + nn(theirs[...], w_sib[:, cols])).astype(BF16)
        for r in range(RING):
            for side in range(2):
                part[j, r, side] = product[r * PIECE : (r + 1) * PIECE, side * HALF : (side + 1) * HALF]
        far(j, 0).start()
        far(j, 1).start()
        near(j, 0).start()
        near(j, 1).start()
        return carry

    lax.fori_loop(0, nchunk, project, 0)

    def forward(j, carry):
        for side in range(2):
            far(j, side).wait_recv()
            slot = (3, 1)[side]
            part[j, slot, side] = (part[j, slot, side].astype(F32) + passed[j, side].astype(F32)).astype(BF16)
            onward(j, side).start()
        return carry

    lax.fori_loop(0, nchunk, forward, 0)

    def finish(j, carry):
        for side in range(2):
            near(j, side).wait_recv()
            onward(j, side).wait_recv()
            cols = pl.ds(pl.multiple_of(j * CHUNK + side * HALF, HALF), HALF)
            out[:, cols] = (
                part[j, 0, side].astype(F32) + direct[j, side].astype(F32) + summed[j, side].astype(F32)
            ).astype(BF16)
        return carry

    lax.fori_loop(0, nchunk, finish, 0)

    def drain(j, carry):
        for side in range(2):
            far(j, side).wait_send()
            near(j, side).wait_send()
            onward(j, side).wait_send()
        return carry

    lax.fori_loop(0, nchunk, drain, 0)
    w_copy.wait_send()
    for copy in swaps:
        copy.wait_send()
    wait_sent(prefixes, two_sem.at[0])


def on_device(queries, keys, values, gate, log_decay, trunc_blocks, norm_gain, w_out):
    nseq = lax.axis_size("seq")
    tokens, width = queries.shape
    columns = w_out.shape[1]
    nchunk, groups = columns // CHUNK, nseq // GROUP
    any_spec = pl.BlockSpec(memory_space=pl.ANY)
    vmem, dma = pltpu.VMEM, pltpu.SemaphoreType.DMA
    return pl.pallas_call(
        functools.partial(kernel, nseq, nchunk, tokens // BLOCK * nseq),
        out_shape=pltpu.VMEM((PIECE, columns), BF16),
        in_specs=[any_spec] * 5 + [pl.BlockSpec(memory_space=pltpu.SMEM)] + [any_spec] * 2,
        out_specs=pl.BlockSpec(memory_space=vmem),
        scratch_shapes=[
            vmem((tokens, width), BF16),
            vmem((tokens, width), BF16),
            vmem((tokens, width), BF16),
            vmem((tokens, width), BF16),
            vmem((2, tokens), BF16),
            vmem((width,), BF16),
            vmem((width, columns), BF16),
            vmem((width, columns), BF16),
            vmem((GROUP, SHARE, DH), BF16),
            vmem((2, DH, DH), F32),
            vmem((2, DH, DH), BF16),
            vmem((2, DH, DH), BF16),
            vmem((2, 1, 128), F32),
            vmem((GROUP, 1, 128), F32),
            vmem((GROUP, SHARE, DH), BF16),
            vmem((GROUP, SHARE, DH), BF16),
            vmem((GROUP, SHARE, DH), BF16),
            vmem((SHARE, DH), BF16),
            vmem((groups, SHARE, DH), BF16),
            vmem((1, 128), F32),
            vmem((groups, 1, 128), F32),
            vmem((tokens, width), F32),
            vmem((tokens, width), F32),
            vmem((2, 2, BLOCK, 128), F32),
            vmem((tokens, width), BF16),
            vmem((RING * PIECE, width), BF16),
            vmem((RING * PIECE, width), BF16),
            vmem((nchunk, RING, 2, PIECE, HALF), BF16),
            vmem((nchunk, 2, PIECE, HALF), BF16),
            vmem((nchunk, 2, PIECE, HALF), BF16),
            vmem((nchunk, 2, PIECE, HALF), BF16),
            dma((7,)),
            dma((2,)),
            dma((2,)),
            dma((2,)),
            dma((2,)),
            dma((groups,)),
            dma((groups,)),
            dma((groups,)),
            dma((groups,)),
            pltpu.SemaphoreType.REGULAR((groups,)),
            pltpu.SemaphoreType.REGULAR,
            dma((2,)),
            dma((2, RING)),
            dma((3, nchunk, 2)),
            dma((3, nchunk, 2)),
        ],
        compiler_params=pltpu.CompilerParams(
            collective_id=0, has_side_effects=True, vmem_limit_bytes=56 * 2**20
        ),
        cost_estimate=pl.CostEstimate(flops=3 * 10**9, bytes_accessed=7 * 2**20, transcendentals=2**20),
    )(queries, keys, values, gate, log_decay, trunc_blocks, norm_gain, w_out)


def solution(mesh):
    in_specs = (
        P("seq", "head"),
        P("seq", "head"),
        P("seq", "head"),
        P("seq", "head"),
        P("head", "seq"),
        P("head"),
        P("head"),
        P("head", None),
    )
    out_specs = P(("seq", "head"), None)
    return jax.shard_map(on_device, mesh=mesh, in_specs=in_specs, out_specs=out_specs, check_vma=False)
```

```python
import functools

import jax
import jax.numpy as jnp
from jax import lax
from jax.experimental import pallas as pl
from jax.experimental.pallas import tpu as pltpu
from jax.sharding import PartitionSpec as P

MESH = pl.DeviceIdType.MESH
F32 = jnp.float32
BF16 = jnp.bfloat16
BLOCK = 256
DH = 256
CHUNK = 512
HALF = CHUNK // 2
PIECE = 64
RING = 4
GROUP = 8
SHARE = 2 * DH // GROUP


def nt(a, b):
    return lax.dot_general(a, b, (((1,), (1,)), ((), ())), preferred_element_type=F32)


def tn(a, b):
    return lax.dot_general(a, b, (((0,), (0,)), ((), ())), preferred_element_type=F32)


def nn(a, b):
    return jnp.dot(a, b, preferred_element_type=F32)


def twice(a):
    return jnp.concatenate([a, a], axis=1)


def kernel(
    nseq, nchunk, steps,
    q_hbm, k_hbm, v_hbm, g_hbm, ld_hbm, trunc, gain_hbm, w_hbm,
    out,
    q, k, v, g, ld, gain, w, w_sib,
    state, first, last, last_in, dec, dec_in, pieces, prefixes, prior, sums, sums_in, fades, fades_in,
    ret, gated, grow, hid, mine, theirs, part, passed, direct, summed,
    load_sem, dec_sem, one_sem, two_sem, last_sem, sum_send, sum_recv, fade_send, fade_recv, ready, ready_last,
    wsib_sem, hid_sem, p_send, p_recv,
):
    seq, head = lax.axis_index("seq"), lax.axis_index("head")
    x, core = lax.div(head, 2), lax.rem(head, 2)
    right = (seq, lax.rem(x + 1, RING) * 2 + core)
    left = (seq, lax.rem(x + RING - 1, RING) * 2 + core)
    sibling = (seq, x * 2 + 1 - core)
    group, place = lax.div(seq, GROUP), lax.rem(seq, GROUP)
    groups = nseq // GROUP
    inside = place < GROUP - 1
    crossing = jnp.logical_and(place == GROUP - 1, group < groups - 1)
    crossed = jnp.logical_and(place == 0, group > 0)

    def fellow(i):
        return group * GROUP + lax.rem(place + i, GROUP)

    def abreast(other):
        return (other * GROUP + place, head)

    barrier = pltpu.get_barrier_semaphore()

    def greet(i, carry):
        pl.semaphore_signal(barrier, inc=1, device_id=(fellow(i), head), device_id_type=MESH)
        return carry

    def greet_later(other, carry):
        pl.semaphore_signal(barrier, inc=1, device_id=abreast(other), device_id_type=MESH)
        return carry

    lax.fori_loop(1, GROUP, greet, 0)
    lax.fori_loop(group + 1, groups, greet_later, 0)

    @pl.when(crossing)
    def _():
        pl.semaphore_signal(barrier, inc=1, device_id=(seq + 1, head), device_id_type=MESH)

    for other in (right, left, sibling):
        pl.semaphore_signal(barrier, inc=1, device_id=other, device_id_type=MESH)

    loads = [
        pltpu.make_async_copy(src, dst, load_sem.at[i])
        for i, (src, dst) in enumerate(
            ((ld_hbm, ld), (k_hbm, k), (v_hbm, v), (q_hbm, q), (g_hbm, g), (gain_hbm, gain), (w_hbm, w))
        )
    ]
    for copy in loads:
        copy.start()

    fast = [trunc[h] < steps for h in range(2)]
    slow_f = [jnp.where(f, 0.0, 1.0).astype(F32) for f in fast]
    lower_i = lax.broadcasted_iota(jnp.int32, (BLOCK, BLOCK), 0)
    lower_j = lax.broadcasted_iota(jnp.int32, (BLOCK, BLOCK), 1)
    causal = lower_j <= lower_i
    tri = jnp.where(causal, 1.0, 0.0).astype(BF16)

    loads[0].wait()
    rates = ld[...].astype(F32)
    down, along, total = {}, {}, {}
    for h in range(2):
        for b in range(2):
            row = jnp.broadcast_to(rates[h : h + 1, b * BLOCK : (b + 1) * BLOCK], (128, BLOCK)).astype(BF16)
            down[h, b] = nt(tri, row)
            along[h, b] = nt(row[:16], tri)[:1]
            total[h, b] = down[h, b][BLOCK - 1 :]
            grow[h, b] = jnp.exp(down[h, b])

    loads[1].wait()
    loads[2].wait()
    for h in range(2):
        cols = pl.ds(h * DH, DH)
        own = []
        for b in range(2):
            rows = pl.ds(b * BLOCK, BLOCK)
            fade = twice(jnp.exp(total[h, b] - down[h, b]))
            own.append(tn((k[rows, cols].astype(F32) * fade).astype(BF16), v[rows, cols]))
        whole = own[0] * twice(jnp.exp(total[h, 1])) + own[1]
        state[pl.ds(h * (GROUP // 2), GROUP // 2)] = whole.astype(BF16).reshape(GROUP // 2, SHARE, DH)
        first[h] = own[0]
        last[h] = own[1].astype(BF16)
        dec[h] = jnp.exp(total[h, 0] + total[h, 1]) * slow_f[h]

    pl.semaphore_wait(barrier, GROUP + 2 + group + jnp.where(crossed, 1, 0))

    def tell(other, carry):
        pl.semaphore_signal(ready.at[group], inc=1, device_id=abreast(other), device_id_type=MESH)
        return carry

    lax.fori_loop(0, group, tell, 0)

    @pl.when(crossed)
    def _():
        pl.semaphore_signal(ready_last, inc=1, device_id=(seq - 1, head), device_id_type=MESH)

    def send_one(i, carry):
        t = lax.rem(place + i, GROUP)
        pltpu.make_async_remote_copy(
            state.at[t], pieces.at[place], one_sem.at[0], one_sem.at[1],
            device_id=(fellow(i), head), device_id_type=MESH,
        ).start()
        return carry

    lax.fori_loop(1, GROUP, send_one, 0)

    def send_dec(i, carry):
        t = lax.rem(place + i, GROUP)
        pltpu.make_async_remote_copy(
            dec.at[lax.div(t, GROUP // 2)], dec_in.at[place], dec_sem.at[0], dec_sem.at[1],
            device_id=(fellow(i), head), device_id_type=MESH,
        ).start()
        return carry

    lax.fori_loop(1, GROUP, send_dec, 0)
    pltpu.make_async_copy(state.at[place], pieces.at[place], one_sem.at[1]).start()
    pltpu.make_async_copy(dec.at[lax.div(place, GROUP // 2)], dec_in.at[place], dec_sem.at[1]).start()

    def last_copy(h):
        return pltpu.make_async_remote_copy(
            last.at[h], last_in.at[h], last_sem.at[0, h], last_sem.at[1, h],
            device_id=(lax.rem(seq + 1, nseq), head), device_id_type=MESH,
        )

    @pl.when(inside)
    def _():
        last_copy(0).start()

    w_copy = pltpu.make_async_remote_copy(
        w_hbm, w_sib, wsib_sem.at[0], wsib_sem.at[1], device_id=sibling, device_id_type=MESH
    )
    w_copy.start()

    loads[3].wait()
    for h in range(2):
        cols = pl.ds(h * DH, DH)
        for b in range(2):
            rows = pl.ds(b * BLOCK, BLOCK)
            decay = jnp.exp(jnp.minimum(twice(down[h, b]) - along[h, b], 0.0))
            weights = jnp.where(causal, nt(q[rows, cols], k[rows, cols]) * decay, 0.0).astype(BF16)
            ret[rows, cols] = nn(weights, v[rows, cols])

    @pl.when(crossing)
    def _():
        pl.semaphore_wait(ready_last, 1)
        last_copy(0).start()

    def wait_all(buffer, sem):
        pltpu.make_async_copy(buffer, buffer, sem).wait()

    def wait_sent(buffer, sem):
        most = buffer.at[pl.ds(0, GROUP - 1)]
        pltpu.make_async_copy(most, most, sem).wait()

    wait_all(dec_in, dec_sem.at[1])
    wait_all(pieces, one_sem.at[1])

    so_far, fade_so_far = jnp.zeros((SHARE, DH), F32), jnp.ones((1, 128), F32)
    for n in range(GROUP):
        so_far = so_far * twice(dec_in[n]) + pieces[n].astype(F32)
        fade_so_far = fade_so_far * dec_in[n]
    sums[...] = so_far.astype(BF16)
    fades[...] = fade_so_far

    def sum_copy(source, target):
        return pltpu.make_async_remote_copy(
            sums, sums_in.at[source], sum_send.at[target], sum_recv.at[source],
            device_id=abreast(target), device_id_type=MESH,
        )

    def fade_copy(source, target):
        return pltpu.make_async_remote_copy(
            fades, fades_in.at[source], fade_send.at[target], fade_recv.at[source],
            device_id=abreast(target), device_id_type=MESH,
        )

    def send_sum(other, carry):
        pl.semaphore_wait(ready.at[other], 1)
        sum_copy(group, other).start()
        fade_copy(group, other).start()
        return carry

    lax.fori_loop(group + 1, groups, send_sum, 0)

    @pl.when(jnp.logical_or(inside, crossing))
    def _():
        last_copy(1).start()

    def add_group(other, total_state):
        fade_copy(other, group).wait_recv()
        sum_copy(other, group).wait_recv()
        return total_state * twice(fades_in[other]) + sums_in[other].astype(F32)

    total_state = lax.fori_loop(0, group, add_group, jnp.zeros((SHARE, DH), F32))

    for n in range(GROUP):
        prefixes[n] = total_state.astype(BF16)
        total_state = total_state * twice(dec_in[n]) + pieces[n].astype(F32)

    def send_two(i, carry):
        t = lax.rem(place + i, GROUP)
        pltpu.make_async_remote_copy(
            prefixes.at[t], prior.at[place], two_sem.at[0], two_sem.at[1],
            device_id=(fellow(i), head), device_id_type=MESH,
        ).start()
        return carry

    lax.fori_loop(1, GROUP, send_two, 0)
    pltpu.make_async_copy(prefixes.at[place], prior.at[place], two_sem.at[1]).start()

    loads[4].wait()
    loads[5].wait()
    gate, width = g[...].astype(F32), g.shape[1]
    gated[...] = gain[...].astype(F32).reshape(1, width) * (gate / (1.0 + jnp.exp(-gate)))
    wait_sent(state, one_sem.at[0])
    wait_sent(dec_in, dec_sem.at[0])

    @pl.when(jnp.logical_or(inside, crossing))
    def _():
        last_copy(0).wait_send()
        last_copy(1).wait_send()

    def sums_sent(other, carry):
        sum_copy(group, other).wait_send()
        fade_copy(group, other).wait_send()
        return carry

    lax.fori_loop(group + 1, groups, sums_sent, 0)
    loads[6].wait()

    @pl.when(seq > 0)
    def _():
        last_copy(0).wait_recv()
        last_copy(1).wait_recv()

    @pl.when(seq == 0)
    def _():
        last_in[...] = jnp.zeros_like(last_in)


    wait_all(prior, two_sem.at[1])
    before = {}
    for h in range(2):
        a = prior[pl.ds(h * (GROUP // 2), GROUP // 2)].reshape(DH, DH)
        near_state = last_in[h].astype(F32) * (1.0 - slow_f[h]) + a.astype(F32) * slow_f[h]
        before[h, 0] = a
        before[h, 1] = (near_state * twice(jnp.exp(total[h, 0])) + first[h]).astype(BF16)
    for b in range(2):
        rows = pl.ds(b * BLOCK, BLOCK)
        for h in range(2):
            cols = pl.ds(h * DH, DH)
            kept = ret[rows, cols] + nn(q[rows, cols], before[h, b]) * twice(grow[h, b])
            mean = jnp.mean(kept, axis=1, keepdims=True)
            centered = kept - mean
            var = jnp.mean(centered * centered, axis=1, keepdims=True)
            hid[rows, cols] = (centered * lax.rsqrt(var + 1e-5) * gated[rows, cols]).astype(BF16)

    def rows_of(r, c):
        return pl.ds(pl.multiple_of((lax.rem(x + r, RING) * 2 + c) * PIECE, PIECE), PIECE)

    swaps = []
    for r in range(RING):
        copy = pltpu.make_async_remote_copy(
            hid.at[rows_of(r, 1 - core)], theirs.at[pl.ds(r * PIECE, PIECE)], hid_sem.at[0, r], hid_sem.at[1, r],
            device_id=sibling, device_id_type=MESH,
        )
        copy.start()
        swaps.append(copy)
    for r in range(RING):
        mine[pl.ds(r * PIECE, PIECE)] = hid[rows_of(r, core)]
    w_copy.wait_recv()
    for copy in swaps:
        copy.wait_recv()

    def push(kind, j, side, src, dst, to):
        return pltpu.make_async_remote_copy(
            src, dst, p_send.at[kind, j, side], p_recv.at[kind, j, side], device_id=to, device_id_type=MESH
        )

    def far(j, side):
        return push(0, j, side, part.at[j, 2, side], passed.at[j, side], (left, right)[side])

    def near(j, side):
        return push(1, j, side, part.at[j, (1, 3)[side], side], direct.at[j, side], (right, left)[side])

    def onward(j, side):
        return push(2, j, side, part.at[j, (3, 1)[side], side], summed.at[j, side], (left, right)[side])

    def project(j, carry):
        cols = pl.ds(pl.multiple_of(j * CHUNK, CHUNK), CHUNK)
        product = (nn(mine[...], w[:, cols]) + nn(theirs[...], w_sib[:, cols])).astype(BF16)
        for r in range(RING):
            for side in range(2):
                part[j, r, side] = product[r * PIECE : (r + 1) * PIECE, side * HALF : (side + 1) * HALF]
        far(j, 0).start()
        far(j, 1).start()
        near(j, 0).start()
        near(j, 1).start()
        return carry

    lax.fori_loop(0, nchunk, project, 0)

    def forward(j, carry):
        for side in range(2):
            far(j, side).wait_recv()
            slot = (3, 1)[side]
            part[j, slot, side] = (part[j, slot, side].astype(F32) + passed[j, side].astype(F32)).astype(BF16)
            onward(j, side).start()
        return carry

    lax.fori_loop(0, nchunk, forward, 0)

    def finish(j, carry):
        for side in range(2):
            near(j, side).wait_recv()
            onward(j, side).wait_recv()
            cols = pl.ds(pl.multiple_of(j * CHUNK + side * HALF, HALF), HALF)
            out[:, cols] = (
                part[j, 0, side].astype(F32) + direct[j, side].astype(F32) + summed[j, side].astype(F32)
            ).astype(BF16)
        return carry

    lax.fori_loop(0, nchunk, finish, 0)

    def drain(j, carry):
        for side in range(2):
            far(j, side).wait_send()
            near(j, side).wait_send()
            onward(j, side).wait_send()
        return carry

    lax.fori_loop(0, nchunk, drain, 0)
    w_copy.wait_send()
    for copy in swaps:
        copy.wait_send()
    wait_sent(prefixes, two_sem.at[0])


def on_device(queries, keys, values, gate, log_decay, trunc_blocks, norm_gain, w_out):
    nseq = lax.axis_size("seq")
    tokens, width = queries.shape
    columns = w_out.shape[1]
    nchunk, groups = columns // CHUNK, nseq // GROUP
    any_spec = pl.BlockSpec(memory_space=pl.ANY)
    vmem, dma = pltpu.VMEM, pltpu.SemaphoreType.DMA
    return pl.pallas_call(
        functools.partial(kernel, nseq, nchunk, tokens // BLOCK * nseq),
        out_shape=pltpu.VMEM((PIECE, columns), BF16),
        in_specs=[any_spec] * 5 + [pl.BlockSpec(memory_space=pltpu.SMEM)] + [any_spec] * 2,
        out_specs=pl.BlockSpec(memory_space=vmem),
        scratch_shapes=[
            vmem((tokens, width), BF16),
            vmem((tokens, width), BF16),
            vmem((tokens, width), BF16),
            vmem((tokens, width), BF16),
            vmem((2, tokens), BF16),
            vmem((width,), BF16),
            vmem((width, columns), BF16),
            vmem((width, columns), BF16),
            vmem((GROUP, SHARE, DH), BF16),
            vmem((2, DH, DH), F32),
            vmem((2, DH, DH), BF16),
            vmem((2, DH, DH), BF16),
            vmem((2, 1, 128), F32),
            vmem((GROUP, 1, 128), F32),
            vmem((GROUP, SHARE, DH), BF16),
            vmem((GROUP, SHARE, DH), BF16),
            vmem((GROUP, SHARE, DH), BF16),
            vmem((SHARE, DH), BF16),
            vmem((groups, SHARE, DH), BF16),
            vmem((1, 128), F32),
            vmem((groups, 1, 128), F32),
            vmem((tokens, width), F32),
            vmem((tokens, width), F32),
            vmem((2, 2, BLOCK, 128), F32),
            vmem((tokens, width), BF16),
            vmem((RING * PIECE, width), BF16),
            vmem((RING * PIECE, width), BF16),
            vmem((nchunk, RING, 2, PIECE, HALF), BF16),
            vmem((nchunk, 2, PIECE, HALF), BF16),
            vmem((nchunk, 2, PIECE, HALF), BF16),
            vmem((nchunk, 2, PIECE, HALF), BF16),
            dma((7,)),
            dma((2,)),
            dma((2,)),
            dma((2,)),
            dma((2, 2)),
            dma((groups,)),
            dma((groups,)),
            dma((groups,)),
            dma((groups,)),
            pltpu.SemaphoreType.REGULAR((groups,)),
            pltpu.SemaphoreType.REGULAR,
            dma((2,)),
            dma((2, RING)),
            dma((3, nchunk, 2)),
            dma((3, nchunk, 2)),
        ],
        compiler_params=pltpu.CompilerParams(
            collective_id=0, has_side_effects=True, vmem_limit_bytes=56 * 2**20
        ),
        cost_estimate=pl.CostEstimate(flops=3 * 10**9, bytes_accessed=7 * 2**20, transcendentals=2**20),
    )(queries, keys, values, gate, log_decay, trunc_blocks, norm_gain, w_out)


def solution(mesh):
    in_specs = (
        P("seq", "head"),
        P("seq", "head"),
        P("seq", "head"),
        P("seq", "head"),
        P("head", "seq"),
        P("head"),
        P("head"),
        P("head", None),
    )
    out_specs = P(("seq", "head"), None)
    return jax.shard_map(on_device, mesh=mesh, in_specs=in_specs, out_specs=out_specs, check_vma=False)
```

```python
import functools

import jax
import jax.numpy as jnp
from jax import lax
from jax.experimental import pallas as pl
from jax.experimental.pallas import tpu as pltpu
from jax.sharding import PartitionSpec as P

MESH = pl.DeviceIdType.MESH
F32 = jnp.float32
BF16 = jnp.bfloat16
BLOCK = 256
DH = 256
CHUNK = 512
HALF = CHUNK // 2
PIECE = 64
RING = 4
GROUP = 8
SHARE = 2 * DH // GROUP


def nt(a, b):
    return lax.dot_general(a, b, (((1,), (1,)), ((), ())), preferred_element_type=F32)


def tn(a, b):
    return lax.dot_general(a, b, (((0,), (0,)), ((), ())), preferred_element_type=F32)


def nn(a, b):
    return jnp.dot(a, b, preferred_element_type=F32)


def twice(a):
    return jnp.concatenate([a, a], axis=1)


def kernel(
    nseq, nchunk, steps,
    q_hbm, k_hbm, v_hbm, g_hbm, ld_hbm, trunc_hbm, gain_hbm, w_hbm,
    out,
    q, k, v, g, ld, trunc, gain, w, w_sib,
    state, first, last, last_in, dec, dec_in, pieces, prefixes, prior, sums, sums_in, fades, fades_in,
    ret, gated, grow, hid, mine, theirs, part, passed, direct, summed,
    load_sem, dec_sem, one_sem, two_sem, last_sem, sum_send, sum_recv, fade_send, fade_recv, ready, ready_last,
    wsib_sem, hid_sem, p_send, p_recv,
):
    seq, head = lax.axis_index("seq"), lax.axis_index("head")
    x, core = lax.div(head, 2), lax.rem(head, 2)
    right = (seq, lax.rem(x + 1, RING) * 2 + core)
    left = (seq, lax.rem(x + RING - 1, RING) * 2 + core)
    sibling = (seq, x * 2 + 1 - core)
    group, place = lax.div(seq, GROUP), lax.rem(seq, GROUP)
    groups = nseq // GROUP
    inside = place < GROUP - 1
    crossing = jnp.logical_and(place == GROUP - 1, group < groups - 1)
    crossed = jnp.logical_and(place == 0, group > 0)

    def fellow(i):
        return group * GROUP + lax.rem(place + i, GROUP)

    def abreast(other):
        return (other * GROUP + place, head)

    barrier = pltpu.get_barrier_semaphore()

    def greet(i, carry):
        pl.semaphore_signal(barrier, inc=1, device_id=(fellow(i), head), device_id_type=MESH)
        return carry

    def greet_later(other, carry):
        pl.semaphore_signal(barrier, inc=1, device_id=abreast(other), device_id_type=MESH)
        return carry

    lax.fori_loop(1, GROUP, greet, 0)
    lax.fori_loop(group + 1, groups, greet_later, 0)

    @pl.when(crossing)
    def _():
        pl.semaphore_signal(barrier, inc=1, device_id=(seq + 1, head), device_id_type=MESH)

    for other in (right, left, sibling):
        pl.semaphore_signal(barrier, inc=1, device_id=other, device_id_type=MESH)

    loads = [
        pltpu.make_async_copy(src, dst, load_sem.at[i])
        for i, (src, dst) in enumerate(
            ((ld_hbm, ld), (k_hbm, k), (v_hbm, v), (q_hbm, q), (g_hbm, g), (gain_hbm, gain), (w_hbm, w), (trunc_hbm, trunc))
        )
    ]
    for copy in loads:
        copy.start()

    loads[7].wait()
    fast = [trunc[h] < steps for h in range(2)]
    slow_f = [jnp.where(f, 0.0, 1.0).astype(F32) for f in fast]
    lower_i = lax.broadcasted_iota(jnp.int32, (BLOCK, BLOCK), 0)
    lower_j = lax.broadcasted_iota(jnp.int32, (BLOCK, BLOCK), 1)
    causal = lower_j <= lower_i
    tri = jnp.where(causal, 1.0, 0.0).astype(BF16)

    loads[0].wait()
    rates = ld[...].astype(F32)
    down, along, total = {}, {}, {}
    for h in range(2):
        for b in range(2):
            row = jnp.broadcast_to(rates[h : h + 1, b * BLOCK : (b + 1) * BLOCK], (128, BLOCK)).astype(BF16)
            down[h, b] = nt(tri, row)
            along[h, b] = nt(row[:16], tri)[:1]
            total[h, b] = down[h, b][BLOCK - 1 :]
            grow[h, b] = jnp.exp(down[h, b])

    loads[1].wait()
    loads[2].wait()
    for h in range(2):
        cols = pl.ds(h * DH, DH)
        own = []
        for b in range(2):
            rows = pl.ds(b * BLOCK, BLOCK)
            fade = twice(jnp.exp(total[h, b] - down[h, b]))
            own.append(tn((k[rows, cols].astype(F32) * fade).astype(BF16), v[rows, cols]))
        whole = own[0] * twice(jnp.exp(total[h, 1])) + own[1]
        state[pl.ds(h * (GROUP // 2), GROUP // 2)] = whole.astype(BF16).reshape(GROUP // 2, SHARE, DH)
        first[h] = own[0]
        last[h] = own[1].astype(BF16)
        dec[h] = jnp.exp(total[h, 0] + total[h, 1]) * slow_f[h]

    pl.semaphore_wait(barrier, GROUP + 2 + group + jnp.where(crossed, 1, 0))

    def tell(other, carry):
        pl.semaphore_signal(ready.at[group], inc=1, device_id=abreast(other), device_id_type=MESH)
        return carry

    lax.fori_loop(0, group, tell, 0)

    @pl.when(crossed)
    def _():
        pl.semaphore_signal(ready_last, inc=1, device_id=(seq - 1, head), device_id_type=MESH)

    def send_one(i, carry):
        t = lax.rem(place + i, GROUP)
        pltpu.make_async_remote_copy(
            state.at[t], pieces.at[place], one_sem.at[0], one_sem.at[1],
            device_id=(fellow(i), head), device_id_type=MESH,
        ).start()
        return carry

    lax.fori_loop(1, GROUP, send_one, 0)

    def send_dec(i, carry):
        t = lax.rem(place + i, GROUP)
        pltpu.make_async_remote_copy(
            dec.at[lax.div(t, GROUP // 2)], dec_in.at[place], dec_sem.at[0], dec_sem.at[1],
            device_id=(fellow(i), head), device_id_type=MESH,
        ).start()
        return carry

    lax.fori_loop(1, GROUP, send_dec, 0)
    pltpu.make_async_copy(state.at[place], pieces.at[place], one_sem.at[1]).start()
    pltpu.make_async_copy(dec.at[lax.div(place, GROUP // 2)], dec_in.at[place], dec_sem.at[1]).start()

    def last_copy(h):
        return pltpu.make_async_remote_copy(
            last.at[h], last_in.at[h], last_sem.at[0, h], last_sem.at[1, h],
            device_id=(lax.rem(seq + 1, nseq), head), device_id_type=MESH,
        )

    @pl.when(inside)
    def _():
        last_copy(0).start()

    w_copy = pltpu.make_async_remote_copy(
        w_hbm, w_sib, wsib_sem.at[0], wsib_sem.at[1], device_id=sibling, device_id_type=MESH
    )
    w_copy.start()

    loads[3].wait()
    for h in range(2):
        cols = pl.ds(h * DH, DH)
        for b in range(2):
            rows = pl.ds(b * BLOCK, BLOCK)
            decay = jnp.exp(jnp.minimum(twice(down[h, b]) - along[h, b], 0.0))
            weights = jnp.where(causal, nt(q[rows, cols], k[rows, cols]) * decay, 0.0).astype(BF16)
            ret[rows, cols] = nn(weights, v[rows, cols])

    @pl.when(crossing)
    def _():
        pl.semaphore_wait(ready_last, 1)
        last_copy(0).start()

    def wait_all(buffer, sem):
        pltpu.make_async_copy(buffer, buffer, sem).wait()

    def wait_sent(buffer, sem):
        most = buffer.at[pl.ds(0, GROUP - 1)]
        pltpu.make_async_copy(most, most, sem).wait()

    wait_all(dec_in, dec_sem.at[1])
    wait_all(pieces, one_sem.at[1])

    so_far, fade_so_far = jnp.zeros((SHARE, DH), F32), jnp.ones((1, 128), F32)
    for n in range(GROUP):
        so_far = so_far * twice(dec_in[n]) + pieces[n].astype(F32)
        fade_so_far = fade_so_far * dec_in[n]
    sums[...] = so_far.astype(BF16)
    fades[...] = fade_so_far

    def sum_copy(source, target):
        return pltpu.make_async_remote_copy(
            sums, sums_in.at[source], sum_send.at[target], sum_recv.at[source],
            device_id=abreast(target), device_id_type=MESH,
        )

    def fade_copy(source, target):
        return pltpu.make_async_remote_copy(
            fades, fades_in.at[source], fade_send.at[target], fade_recv.at[source],
            device_id=abreast(target), device_id_type=MESH,
        )

    def send_sum(other, carry):
        pl.semaphore_wait(ready.at[other], 1)
        sum_copy(group, other).start()
        fade_copy(group, other).start()
        return carry

    lax.fori_loop(group + 1, groups, send_sum, 0)

    @pl.when(jnp.logical_or(inside, crossing))
    def _():
        last_copy(1).start()

    def add_group(other, total_state):
        fade_copy(other, group).wait_recv()
        sum_copy(other, group).wait_recv()
        return total_state * twice(fades_in[other]) + sums_in[other].astype(F32)

    total_state = lax.fori_loop(0, group, add_group, jnp.zeros((SHARE, DH), F32))

    for n in range(GROUP):
        prefixes[n] = total_state.astype(BF16)
        total_state = total_state * twice(dec_in[n]) + pieces[n].astype(F32)

    def send_two(i, carry):
        t = lax.rem(place + i, GROUP)
        pltpu.make_async_remote_copy(
            prefixes.at[t], prior.at[place], two_sem.at[0], two_sem.at[1],
            device_id=(fellow(i), head), device_id_type=MESH,
        ).start()
        return carry

    lax.fori_loop(1, GROUP, send_two, 0)
    pltpu.make_async_copy(prefixes.at[place], prior.at[place], two_sem.at[1]).start()

    loads[4].wait()
    loads[5].wait()
    gate, width = g[...].astype(F32), g.shape[1]
    gated[...] = gain[...].astype(F32).reshape(1, width) * (gate / (1.0 + jnp.exp(-gate)))
    wait_sent(state, one_sem.at[0])
    wait_sent(dec_in, dec_sem.at[0])

    @pl.when(jnp.logical_or(inside, crossing))
    def _():
        last_copy(0).wait_send()
        last_copy(1).wait_send()

    def sums_sent(other, carry):
        sum_copy(group, other).wait_send()
        fade_copy(group, other).wait_send()
        return carry

    lax.fori_loop(group + 1, groups, sums_sent, 0)
    loads[6].wait()

    @pl.when(seq > 0)
    def _():
        last_copy(0).wait_recv()
        last_copy(1).wait_recv()

    @pl.when(seq == 0)
    def _():
        last_in[...] = jnp.zeros_like(last_in)


    wait_all(prior, two_sem.at[1])
    before = {}
    for h in range(2):
        a = prior[pl.ds(h * (GROUP // 2), GROUP // 2)].reshape(DH, DH)
        near_state = last_in[h].astype(F32) * (1.0 - slow_f[h]) + a.astype(F32) * slow_f[h]
        before[h, 0] = a
        before[h, 1] = (near_state * twice(jnp.exp(total[h, 0])) + first[h]).astype(BF16)
    for b in range(2):
        rows = pl.ds(b * BLOCK, BLOCK)
        for h in range(2):
            cols = pl.ds(h * DH, DH)
            kept = ret[rows, cols] + nn(q[rows, cols], before[h, b]) * twice(grow[h, b])
            mean = jnp.mean(kept, axis=1, keepdims=True)
            centered = kept - mean
            var = jnp.mean(centered * centered, axis=1, keepdims=True)
            hid[rows, cols] = (centered * lax.rsqrt(var + 1e-5) * gated[rows, cols]).astype(BF16)

    def rows_of(r, c):
        return pl.ds(pl.multiple_of((lax.rem(x + r, RING) * 2 + c) * PIECE, PIECE), PIECE)

    swaps = []
    for r in range(RING):
        copy = pltpu.make_async_remote_copy(
            hid.at[rows_of(r, 1 - core)], theirs.at[pl.ds(r * PIECE, PIECE)], hid_sem.at[0, r], hid_sem.at[1, r],
            device_id=sibling, device_id_type=MESH,
        )
        copy.start()
        swaps.append(copy)
    for r in range(RING):
        mine[pl.ds(r * PIECE, PIECE)] = hid[rows_of(r, core)]
    w_copy.wait_recv()
    for copy in swaps:
        copy.wait_recv()

    def push(kind, j, side, src, dst, to):
        return pltpu.make_async_remote_copy(
            src, dst, p_send.at[kind, j, side], p_recv.at[kind, j, side], device_id=to, device_id_type=MESH
        )

    def far(j, side):
        return push(0, j, side, part.at[j, 2, side], passed.at[j, side], (left, right)[side])

    def near(j, side):
        return push(1, j, side, part.at[j, (1, 3)[side], side], direct.at[j, side], (right, left)[side])

    def onward(j, side):
        return push(2, j, side, part.at[j, (3, 1)[side], side], summed.at[j, side], (left, right)[side])

    def project(j, carry):
        cols = pl.ds(pl.multiple_of(j * CHUNK, CHUNK), CHUNK)
        product = (nn(mine[...], w[:, cols]) + nn(theirs[...], w_sib[:, cols])).astype(BF16)
        for r in range(RING):
            for side in range(2):
                part[j, r, side] = product[r * PIECE : (r + 1) * PIECE, side * HALF : (side + 1) * HALF]
        far(j, 0).start()
        far(j, 1).start()
        near(j, 0).start()
        near(j, 1).start()
        return carry

    lax.fori_loop(0, nchunk, project, 0)

    def forward(j, carry):
        for side in range(2):
            far(j, side).wait_recv()
            slot = (3, 1)[side]
            part[j, slot, side] = (part[j, slot, side].astype(F32) + passed[j, side].astype(F32)).astype(BF16)
            onward(j, side).start()
        return carry

    lax.fori_loop(0, nchunk, forward, 0)

    def finish(j, carry):
        for side in range(2):
            near(j, side).wait_recv()
            onward(j, side).wait_recv()
            cols = pl.ds(pl.multiple_of(j * CHUNK + side * HALF, HALF), HALF)
            out[:, cols] = (
                part[j, 0, side].astype(F32) + direct[j, side].astype(F32) + summed[j, side].astype(F32)
            ).astype(BF16)
        return carry

    lax.fori_loop(0, nchunk, finish, 0)

    def drain(j, carry):
        for side in range(2):
            far(j, side).wait_send()
            near(j, side).wait_send()
            onward(j, side).wait_send()
        return carry

    lax.fori_loop(0, nchunk, drain, 0)
    w_copy.wait_send()
    for copy in swaps:
        copy.wait_send()
    wait_sent(prefixes, two_sem.at[0])


def on_device(queries, keys, values, gate, log_decay, trunc_blocks, norm_gain, w_out):
    nseq = lax.axis_size("seq")
    tokens, width = queries.shape
    columns = w_out.shape[1]
    nchunk, groups = columns // CHUNK, nseq // GROUP
    any_spec = pl.BlockSpec(memory_space=pl.ANY)
    vmem, dma = pltpu.VMEM, pltpu.SemaphoreType.DMA
    return pl.pallas_call(
        functools.partial(kernel, nseq, nchunk, tokens // BLOCK * nseq),
        out_shape=pltpu.VMEM((PIECE, columns), BF16),
        in_specs=[any_spec] * 8,
        out_specs=pl.BlockSpec(memory_space=vmem),
        scratch_shapes=[
            vmem((tokens, width), BF16),
            vmem((tokens, width), BF16),
            vmem((tokens, width), BF16),
            vmem((tokens, width), BF16),
            vmem((2, tokens), BF16),
            pltpu.SMEM((2,), jnp.int32),
            vmem((width,), BF16),
            vmem((width, columns), BF16),
            vmem((width, columns), BF16),
            vmem((GROUP, SHARE, DH), BF16),
            vmem((2, DH, DH), F32),
            vmem((2, DH, DH), BF16),
            vmem((2, DH, DH), BF16),
            vmem((2, 1, 128), F32),
            vmem((GROUP, 1, 128), F32),
            vmem((GROUP, SHARE, DH), BF16),
            vmem((GROUP, SHARE, DH), BF16),
            vmem((GROUP, SHARE, DH), BF16),
            vmem((SHARE, DH), BF16),
            vmem((groups, SHARE, DH), BF16),
            vmem((1, 128), F32),
            vmem((groups, 1, 128), F32),
            vmem((tokens, width), F32),
            vmem((tokens, width), F32),
            vmem((2, 2, BLOCK, 128), F32),
            vmem((tokens, width), BF16),
            vmem((RING * PIECE, width), BF16),
            vmem((RING * PIECE, width), BF16),
            vmem((nchunk, RING, 2, PIECE, HALF), BF16),
            vmem((nchunk, 2, PIECE, HALF), BF16),
            vmem((nchunk, 2, PIECE, HALF), BF16),
            vmem((nchunk, 2, PIECE, HALF), BF16),
            dma((8,)),
            dma((2,)),
            dma((2,)),
            dma((2,)),
            dma((2, 2)),
            dma((groups,)),
            dma((groups,)),
            dma((groups,)),
            dma((groups,)),
            pltpu.SemaphoreType.REGULAR((groups,)),
            pltpu.SemaphoreType.REGULAR,
            dma((2,)),
            dma((2, RING)),
            dma((3, nchunk, 2)),
            dma((3, nchunk, 2)),
        ],
        compiler_params=pltpu.CompilerParams(
            collective_id=0, has_side_effects=True, vmem_limit_bytes=56 * 2**20
        ),
        cost_estimate=pl.CostEstimate(flops=3 * 10**9, bytes_accessed=7 * 2**20, transcendentals=2**20),
    )(queries, keys, values, gate, log_decay, trunc_blocks, norm_gain, w_out)


def solution(mesh):
    in_specs = (
        P("seq", "head"),
        P("seq", "head"),
        P("seq", "head"),
        P("seq", "head"),
        P("head", "seq"),
        P("head"),
        P("head"),
        P("head", None),
    )
    out_specs = P(("seq", "head"), None)
    return jax.shard_map(on_device, mesh=mesh, in_specs=in_specs, out_specs=out_specs, check_vma=False)
```

```python
import functools

import jax
import jax.numpy as jnp
from jax import lax
from jax.experimental import pallas as pl
from jax.experimental.pallas import tpu as pltpu
from jax.sharding import PartitionSpec as P

MESH = pl.DeviceIdType.MESH
F32 = jnp.float32
BF16 = jnp.bfloat16
BLOCK = 256
DH = 256
CHUNK = 1024
HALF = CHUNK // 2
PIECE = 64
RING = 4
GROUP = 8
SHARE = 2 * DH // GROUP


def nt(a, b):
    return lax.dot_general(a, b, (((1,), (1,)), ((), ())), preferred_element_type=F32)


def tn(a, b):
    return lax.dot_general(a, b, (((0,), (0,)), ((), ())), preferred_element_type=F32)


def nn(a, b):
    return jnp.dot(a, b, preferred_element_type=F32)


def twice(a):
    return jnp.concatenate([a, a], axis=1)


def kernel(
    nseq, nchunk, steps,
    q_hbm, k_hbm, v_hbm, g_hbm, ld_hbm, trunc_hbm, gain_hbm, w_hbm,
    out,
    q, k, v, g, ld, trunc, gain, w, w_sib,
    state, first, last, last_in, dec, dec_in, pieces, prefixes, prior, sums, sums_in, fades, fades_in,
    ret, gated, grow, hid, mine, theirs, part, passed, direct, summed, own,
    load_sem, dec_sem, one_sem, two_sem, last_sem, sum_send, sum_recv, fade_send, fade_recv, ready, ready_last,
    wsib_sem, hid_sem, p_send, p_recv,
):
    seq, head = lax.axis_index("seq"), lax.axis_index("head")
    x, core = lax.div(head, 2), lax.rem(head, 2)
    right = (seq, lax.rem(x + 1, RING) * 2 + core)
    left = (seq, lax.rem(x + RING - 1, RING) * 2 + core)
    sibling = (seq, x * 2 + 1 - core)
    group, place = lax.div(seq, GROUP), lax.rem(seq, GROUP)
    groups = nseq // GROUP
    inside = place < GROUP - 1
    crossing = jnp.logical_and(place == GROUP - 1, group < groups - 1)
    crossed = jnp.logical_and(place == 0, group > 0)

    def fellow(i):
        return group * GROUP + lax.rem(place + i, GROUP)

    def abreast(other):
        return (other * GROUP + place, head)

    barrier = pltpu.get_barrier_semaphore()

    def greet(i, carry):
        pl.semaphore_signal(barrier, inc=1, device_id=(fellow(i), head), device_id_type=MESH)
        return carry

    def greet_later(other, carry):
        pl.semaphore_signal(barrier, inc=1, device_id=abreast(other), device_id_type=MESH)
        return carry

    lax.fori_loop(1, GROUP, greet, 0)
    lax.fori_loop(group + 1, groups, greet_later, 0)

    @pl.when(crossing)
    def _():
        pl.semaphore_signal(barrier, inc=1, device_id=(seq + 1, head), device_id_type=MESH)

    for other in (right, left, sibling):
        pl.semaphore_signal(barrier, inc=1, device_id=other, device_id_type=MESH)

    loads = [
        pltpu.make_async_copy(src, dst, load_sem.at[i])
        for i, (src, dst) in enumerate(
            ((ld_hbm, ld), (k_hbm, k), (v_hbm, v), (q_hbm, q), (g_hbm, g), (gain_hbm, gain), (w_hbm, w), (trunc_hbm, trunc))
        )
    ]
    for copy in loads:
        copy.start()

    loads[7].wait()
    fast = [trunc[h] < steps for h in range(2)]
    slow_f = [jnp.where(f, 0.0, 1.0).astype(F32) for f in fast]
    lower_i = lax.broadcasted_iota(jnp.int32, (BLOCK, BLOCK), 0)
    lower_j = lax.broadcasted_iota(jnp.int32, (BLOCK, BLOCK), 1)
    causal = lower_j <= lower_i
    tri = jnp.where(causal, 1.0, 0.0).astype(BF16)

    loads[0].wait()
    rates = ld[...].astype(F32)
    down, along, total = {}, {}, {}
    for h in range(2):
        for b in range(2):
            row = jnp.broadcast_to(rates[h : h + 1, b * BLOCK : (b + 1) * BLOCK], (128, BLOCK)).astype(BF16)
            down[h, b] = nt(tri, row)
            along[h, b] = nt(row[:16], tri)[:1]
            total[h, b] = down[h, b][BLOCK - 1 :]
            grow[h, b] = jnp.exp(down[h, b])

    loads[1].wait()
    loads[2].wait()
    for h in range(2):
        cols = pl.ds(h * DH, DH)
        states = []
        for b in range(2):
            rows = pl.ds(b * BLOCK, BLOCK)
            fade = twice(jnp.exp(total[h, b] - down[h, b]))
            states.append(tn((k[rows, cols].astype(F32) * fade).astype(BF16), v[rows, cols]))
        whole = states[0] * twice(jnp.exp(total[h, 1])) + states[1]
        state[pl.ds(h * (GROUP // 2), GROUP // 2)] = whole.astype(BF16).reshape(GROUP // 2, SHARE, DH)
        first[h] = states[0]
        last[h] = states[1].astype(BF16)
        dec[h] = jnp.exp(total[h, 0] + total[h, 1]) * slow_f[h]

    pl.semaphore_wait(barrier, GROUP + 2 + group + jnp.where(crossed, 1, 0))

    def tell(other, carry):
        pl.semaphore_signal(ready.at[group], inc=1, device_id=abreast(other), device_id_type=MESH)
        return carry

    lax.fori_loop(0, group, tell, 0)

    @pl.when(crossed)
    def _():
        pl.semaphore_signal(ready_last, inc=1, device_id=(seq - 1, head), device_id_type=MESH)

    def send_one(i, carry):
        t = lax.rem(place + i, GROUP)
        pltpu.make_async_remote_copy(
            state.at[t], pieces.at[place], one_sem.at[0], one_sem.at[1],
            device_id=(fellow(i), head), device_id_type=MESH,
        ).start()
        return carry

    lax.fori_loop(1, GROUP, send_one, 0)

    def send_dec(i, carry):
        t = lax.rem(place + i, GROUP)
        pltpu.make_async_remote_copy(
            dec.at[lax.div(t, GROUP // 2)], dec_in.at[place], dec_sem.at[0], dec_sem.at[1],
            device_id=(fellow(i), head), device_id_type=MESH,
        ).start()
        return carry

    lax.fori_loop(1, GROUP, send_dec, 0)
    pltpu.make_async_copy(state.at[place], pieces.at[place], one_sem.at[1]).start()
    pltpu.make_async_copy(dec.at[lax.div(place, GROUP // 2)], dec_in.at[place], dec_sem.at[1]).start()

    def last_copy(h):
        return pltpu.make_async_remote_copy(
            last.at[h], last_in.at[h], last_sem.at[0, h], last_sem.at[1, h],
            device_id=(lax.rem(seq + 1, nseq), head), device_id_type=MESH,
        )

    @pl.when(inside)
    def _():
        last_copy(0).start()

    w_copy = pltpu.make_async_remote_copy(
        w_hbm, w_sib, wsib_sem.at[0], wsib_sem.at[1], device_id=sibling, device_id_type=MESH
    )
    w_copy.start()

    loads[3].wait()
    for h in range(2):
        cols = pl.ds(h * DH, DH)
        for b in range(2):
            rows = pl.ds(b * BLOCK, BLOCK)
            decay = jnp.exp(jnp.minimum(twice(down[h, b]) - along[h, b], 0.0))
            weights = jnp.where(causal, nt(q[rows, cols], k[rows, cols]) * decay, 0.0).astype(BF16)
            ret[rows, cols] = nn(weights, v[rows, cols])

    @pl.when(crossing)
    def _():
        pl.semaphore_wait(ready_last, 1)
        last_copy(0).start()

    def wait_all(buffer, sem):
        pltpu.make_async_copy(buffer, buffer, sem).wait()

    def wait_sent(buffer, sem):
        most = buffer.at[pl.ds(0, GROUP - 1)]
        pltpu.make_async_copy(most, most, sem).wait()

    wait_all(dec_in, dec_sem.at[1])
    wait_all(pieces, one_sem.at[1])

    so_far, fade_so_far = jnp.zeros((SHARE, DH), F32), jnp.ones((1, 128), F32)
    for n in range(GROUP):
        so_far = so_far * twice(dec_in[n]) + pieces[n].astype(F32)
        fade_so_far = fade_so_far * dec_in[n]
    sums[...] = so_far.astype(BF16)
    fades[...] = fade_so_far

    def sum_copy(source, target):
        return pltpu.make_async_remote_copy(
            sums, sums_in.at[source], sum_send.at[target], sum_recv.at[source],
            device_id=abreast(target), device_id_type=MESH,
        )

    def fade_copy(source, target):
        return pltpu.make_async_remote_copy(
            fades, fades_in.at[source], fade_send.at[target], fade_recv.at[source],
            device_id=abreast(target), device_id_type=MESH,
        )

    def send_sum(other, carry):
        pl.semaphore_wait(ready.at[other], 1)
        sum_copy(group, other).start()
        fade_copy(group, other).start()
        return carry

    lax.fori_loop(group + 1, groups, send_sum, 0)

    @pl.when(jnp.logical_or(inside, crossing))
    def _():
        last_copy(1).start()

    def add_group(other, total_state):
        fade_copy(other, group).wait_recv()
        sum_copy(other, group).wait_recv()
        return total_state * twice(fades_in[other]) + sums_in[other].astype(F32)

    total_state = lax.fori_loop(0, group, add_group, jnp.zeros((SHARE, DH), F32))

    for n in range(GROUP):
        prefixes[n] = total_state.astype(BF16)
        total_state = total_state * twice(dec_in[n]) + pieces[n].astype(F32)

    def send_two(i, carry):
        t = lax.rem(place + i, GROUP)
        pltpu.make_async_remote_copy(
            prefixes.at[t], prior.at[place], two_sem.at[0], two_sem.at[1],
            device_id=(fellow(i), head), device_id_type=MESH,
        ).start()
        return carry

    lax.fori_loop(1, GROUP, send_two, 0)
    pltpu.make_async_copy(prefixes.at[place], prior.at[place], two_sem.at[1]).start()

    loads[4].wait()
    loads[5].wait()
    gate, width = g[...].astype(F32), g.shape[1]
    gated[...] = gain[...].astype(F32).reshape(1, width) * (gate / (1.0 + jnp.exp(-gate)))
    wait_sent(state, one_sem.at[0])
    wait_sent(dec_in, dec_sem.at[0])

    @pl.when(jnp.logical_or(inside, crossing))
    def _():
        last_copy(0).wait_send()
        last_copy(1).wait_send()

    def sums_sent(other, carry):
        sum_copy(group, other).wait_send()
        fade_copy(group, other).wait_send()
        return carry

    lax.fori_loop(group + 1, groups, sums_sent, 0)
    loads[6].wait()

    @pl.when(seq > 0)
    def _():
        last_copy(0).wait_recv()
        last_copy(1).wait_recv()

    @pl.when(seq == 0)
    def _():
        last_in[...] = jnp.zeros_like(last_in)


    wait_all(prior, two_sem.at[1])
    before = {}
    for h in range(2):
        a = prior[pl.ds(h * (GROUP // 2), GROUP // 2)].reshape(DH, DH)
        near_state = last_in[h].astype(F32) * (1.0 - slow_f[h]) + a.astype(F32) * slow_f[h]
        before[h, 0] = a
        before[h, 1] = (near_state * twice(jnp.exp(total[h, 0])) + first[h]).astype(BF16)
    for b in range(2):
        rows = pl.ds(b * BLOCK, BLOCK)
        for h in range(2):
            cols = pl.ds(h * DH, DH)
            kept = ret[rows, cols] + nn(q[rows, cols], before[h, b]) * twice(grow[h, b])
            mean = jnp.mean(kept, axis=1, keepdims=True)
            centered = kept - mean
            var = jnp.mean(centered * centered, axis=1, keepdims=True)
            hid[rows, cols] = (centered * lax.rsqrt(var + 1e-5) * gated[rows, cols]).astype(BF16)

    def rows_of(r, c):
        return pl.ds(pl.multiple_of((lax.rem(x + r, RING) * 2 + c) * PIECE, PIECE), PIECE)

    swaps = []
    for r in range(RING):
        copy = pltpu.make_async_remote_copy(
            hid.at[rows_of(r, 1 - core)], theirs.at[pl.ds(r * PIECE, PIECE)], hid_sem.at[0, r], hid_sem.at[1, r],
            device_id=sibling, device_id_type=MESH,
        )
        copy.start()
        swaps.append(copy)
    for r in range(RING):
        mine[pl.ds(r * PIECE, PIECE)] = hid[rows_of(r, core)]
    w_copy.wait_recv()
    for copy in swaps:
        copy.wait_recv()

    def push(kind, j, side, src, dst, to):
        return pltpu.make_async_remote_copy(
            src, dst, p_send.at[kind, j, side], p_recv.at[kind, j, side], device_id=to, device_id_type=MESH
        )

    def far(j, side):
        return push(0, j, side, part.at[j, 2, side], passed.at[j, side], (left, right)[side])

    def near(j, side):
        return push(1, j, side, part.at[j, (1, 3)[side], side], direct.at[j, side], (right, left)[side])

    def onward(j, side):
        return push(2, j, side, part.at[j, (3, 1)[side], side], summed.at[j, side], (left, right)[side])

    def project(j, carry):
        cols = pl.ds(pl.multiple_of(j * CHUNK, CHUNK), CHUNK)
        product = (nn(mine[...], w[:, cols]) + nn(theirs[...], w_sib[:, cols])).astype(BF16)
        for r in range(RING):
            for side in range(2):
                part[j, r, side] = product[r * PIECE : (r + 1) * PIECE, side * HALF : (side + 1) * HALF]
        far(j, 0).start()
        far(j, 1).start()
        near(j, 0).start()
        near(j, 1).start()
        return carry

    lax.fori_loop(0, nchunk, project, 0)

    def forward(j, carry):
        for side in range(2):
            far(j, side).wait_recv()
            slot = (3, 1)[side]
            part[j, slot, side] = (part[j, slot, side].astype(F32) + passed[j, side].astype(F32)).astype(BF16)
            onward(j, side).start()
        return carry

    lax.fori_loop(0, nchunk, forward, 0)

    w_copy.wait_send()
    for copy in swaps:
        copy.wait_send()
    wait_sent(prefixes, two_sem.at[0])

    def gather(j, carry):
        for side in range(2):
            far(j, side).wait_send()
            near(j, side).wait_send()
            near(j, side).wait_recv()
            own[j, side] = part[j, 0, side].astype(F32) + direct[j, side].astype(F32)
        return carry

    def finish(j, carry):
        for side in range(2):
            onward(j, side).wait_recv()
            cols = pl.ds(pl.multiple_of(j * CHUNK + side * HALF, HALF), HALF)
            out[:, cols] = (own[j, side] + summed[j, side].astype(F32)).astype(BF16)
            onward(j, side).wait_send()
        return carry

    lax.fori_loop(0, nchunk, gather, 0)
    lax.fori_loop(0, nchunk, finish, 0)


def on_device(queries, keys, values, gate, log_decay, trunc_blocks, norm_gain, w_out):
    nseq = lax.axis_size("seq")
    tokens, width = queries.shape
    columns = w_out.shape[1]
    nchunk, groups = columns // CHUNK, nseq // GROUP
    any_spec = pl.BlockSpec(memory_space=pl.ANY)
    vmem, dma = pltpu.VMEM, pltpu.SemaphoreType.DMA
    return pl.pallas_call(
        functools.partial(kernel, nseq, nchunk, tokens // BLOCK * nseq),
        out_shape=pltpu.VMEM((PIECE, columns), BF16),
        in_specs=[any_spec] * 8,
        out_specs=pl.BlockSpec(memory_space=vmem),
        scratch_shapes=[
            vmem((tokens, width), BF16),
            vmem((tokens, width), BF16),
            vmem((tokens, width), BF16),
            vmem((tokens, width), BF16),
            vmem((2, tokens), BF16),
            pltpu.SMEM((2,), jnp.int32),
            vmem((width,), BF16),
            vmem((width, columns), BF16),
            vmem((width, columns), BF16),
            vmem((GROUP, SHARE, DH), BF16),
            vmem((2, DH, DH), F32),
            vmem((2, DH, DH), BF16),
            vmem((2, DH, DH), BF16),
            vmem((2, 1, 128), F32),
            vmem((GROUP, 1, 128), F32),
            vmem((GROUP, SHARE, DH), BF16),
            vmem((GROUP, SHARE, DH), BF16),
            vmem((GROUP, SHARE, DH), BF16),
            vmem((SHARE, DH), BF16),
            vmem((groups, SHARE, DH), BF16),
            vmem((1, 128), F32),
            vmem((groups, 1, 128), F32),
            vmem((tokens, width), F32),
            vmem((tokens, width), F32),
            vmem((2, 2, BLOCK, 128), F32),
            vmem((tokens, width), BF16),
            vmem((RING * PIECE, width), BF16),
            vmem((RING * PIECE, width), BF16),
            vmem((nchunk, RING, 2, PIECE, HALF), BF16),
            vmem((nchunk, 2, PIECE, HALF), BF16),
            vmem((nchunk, 2, PIECE, HALF), BF16),
            vmem((nchunk, 2, PIECE, HALF), BF16),
            vmem((nchunk, 2, PIECE, HALF), F32),
            dma((8,)),
            dma((2,)),
            dma((2,)),
            dma((2,)),
            dma((2, 2)),
            dma((groups,)),
            dma((groups,)),
            dma((groups,)),
            dma((groups,)),
            pltpu.SemaphoreType.REGULAR((groups,)),
            pltpu.SemaphoreType.REGULAR,
            dma((2,)),
            dma((2, RING)),
            dma((3, nchunk, 2)),
            dma((3, nchunk, 2)),
        ],
        compiler_params=pltpu.CompilerParams(
            collective_id=0, has_side_effects=True, vmem_limit_bytes=56 * 2**20
        ),
        cost_estimate=pl.CostEstimate(flops=3 * 10**9, bytes_accessed=7 * 2**20, transcendentals=2**20),
    )(queries, keys, values, gate, log_decay, trunc_blocks, norm_gain, w_out)


def solution(mesh):
    in_specs = (
        P("seq", "head"),
        P("seq", "head"),
        P("seq", "head"),
        P("seq", "head"),
        P("head", "seq"),
        P("head"),
        P("head"),
        P("head", None),
    )
    out_specs = P(("seq", "head"), None)
    return jax.shard_map(on_device, mesh=mesh, in_specs=in_specs, out_specs=out_specs, check_vma=False)
```

```python
import functools

import jax
import jax.numpy as jnp
from jax import lax
from jax.experimental import pallas as pl
from jax.experimental.pallas import tpu as pltpu
from jax.sharding import PartitionSpec as P

MESH = pl.DeviceIdType.MESH
F32 = jnp.float32
BF16 = jnp.bfloat16
BLOCK = 256
DH = 256
CHUNK = 1024
HALF = CHUNK // 2
PIECE = 64
RING = 4
GROUP = 8
SHARE = 2 * DH // GROUP


def nt(a, b):
    return lax.dot_general(a, b, (((1,), (1,)), ((), ())), preferred_element_type=F32)


def tn(a, b):
    return lax.dot_general(a, b, (((0,), (0,)), ((), ())), preferred_element_type=F32)


def nn(a, b):
    return jnp.dot(a, b, preferred_element_type=F32)


def twice(a):
    return jnp.concatenate([a, a], axis=1)


def kernel(
    nseq, nchunk, steps,
    q_hbm, k_hbm, v_hbm, g_hbm, ld_hbm, trunc_hbm, gain_hbm, w_hbm,
    out,
    q, k, v, g, ld, trunc, gain, w, w_sib,
    state, first, last, last_in, dec, dec_in, pieces, prefixes, prior, sums, sums_in, fades, fades_in,
    ret, gated, grow, hid, mine, theirs, part, passed, direct, summed, own,
    load_sem, dec_sem, one_sem, two_sem, last_sem, sum_send, sum_recv, fade_send, fade_recv, ready, ready_last,
    wsib_sem, hid_sem, p_send, p_recv,
):
    seq, head = lax.axis_index("seq"), lax.axis_index("head")
    x, core = lax.div(head, 2), lax.rem(head, 2)
    right = (seq, lax.rem(x + 1, RING) * 2 + core)
    left = (seq, lax.rem(x + RING - 1, RING) * 2 + core)
    sibling = (seq, x * 2 + 1 - core)
    group, place = lax.div(seq, GROUP), lax.rem(seq, GROUP)
    groups = nseq // GROUP
    inside = place < GROUP - 1
    crossing = jnp.logical_and(place == GROUP - 1, group < groups - 1)
    crossed = jnp.logical_and(place == 0, group > 0)

    def fellow(i):
        return group * GROUP + lax.rem(place + i, GROUP)

    def abreast(other):
        return (other * GROUP + place, head)

    barrier = pltpu.get_barrier_semaphore()

    def greet(i, carry):
        pl.semaphore_signal(barrier, inc=1, device_id=(fellow(i), head), device_id_type=MESH)
        return carry

    def greet_later(other, carry):
        pl.semaphore_signal(barrier, inc=1, device_id=abreast(other), device_id_type=MESH)
        return carry

    lax.fori_loop(1, GROUP, greet, 0)
    lax.fori_loop(group + 1, groups, greet_later, 0)

    @pl.when(crossing)
    def _():
        pl.semaphore_signal(barrier, inc=1, device_id=(seq + 1, head), device_id_type=MESH)

    for other in (right, left, sibling):
        pl.semaphore_signal(barrier, inc=1, device_id=other, device_id_type=MESH)

    loads = [
        pltpu.make_async_copy(src, dst, load_sem.at[i])
        for i, (src, dst) in enumerate(
            ((ld_hbm, ld), (k_hbm, k), (v_hbm, v), (q_hbm, q), (g_hbm, g), (gain_hbm, gain), (w_hbm, w), (trunc_hbm, trunc))
        )
    ]
    for copy in loads:
        copy.start()

    loads[7].wait()
    fast = [trunc[h] < steps for h in range(2)]
    slow_f = [jnp.where(f, 0.0, 1.0).astype(F32) for f in fast]
    lower_i = lax.broadcasted_iota(jnp.int32, (BLOCK, BLOCK), 0)
    lower_j = lax.broadcasted_iota(jnp.int32, (BLOCK, BLOCK), 1)
    causal = lower_j <= lower_i
    tri = jnp.where(causal, 1.0, 0.0).astype(BF16)

    loads[0].wait()
    rates = ld[...].astype(F32)
    down, along, total = {}, {}, {}
    for h in range(2):
        for b in range(2):
            row = jnp.broadcast_to(rates[h : h + 1, b * BLOCK : (b + 1) * BLOCK], (128, BLOCK)).astype(BF16)
            down[h, b] = nt(tri, row)
            along[h, b] = nt(row[:16], tri)[:1]
            total[h, b] = down[h, b][BLOCK - 1 :]
            grow[h, b] = jnp.exp(down[h, b])

    loads[1].wait()
    loads[2].wait()
    for h in range(2):
        cols = pl.ds(h * DH, DH)
        states = []
        for b in range(2):
            rows = pl.ds(b * BLOCK, BLOCK)
            fade = twice(jnp.exp(total[h, b] - down[h, b]))
            states.append(tn((k[rows, cols].astype(F32) * fade).astype(BF16), v[rows, cols]))
        whole = states[0] * twice(jnp.exp(total[h, 1])) + states[1]
        state[pl.ds(h * (GROUP // 2), GROUP // 2)] = whole.astype(BF16).reshape(GROUP // 2, SHARE, DH)
        first[h] = states[0]
        last[h] = states[1].astype(BF16)
        dec[h] = jnp.exp(total[h, 0] + total[h, 1]) * slow_f[h]

    pl.semaphore_wait(barrier, GROUP + 2 + group + jnp.where(crossed, 1, 0))

    def tell(other, carry):
        pl.semaphore_signal(ready.at[group], inc=1, device_id=abreast(other), device_id_type=MESH)
        return carry

    lax.fori_loop(0, group, tell, 0)

    @pl.when(crossed)
    def _():
        pl.semaphore_signal(ready_last, inc=1, device_id=(seq - 1, head), device_id_type=MESH)

    def send_one(i, carry):
        t = lax.rem(place + i, GROUP)
        pltpu.make_async_remote_copy(
            state.at[t], pieces.at[place], one_sem.at[0], one_sem.at[1],
            device_id=(fellow(i), head), device_id_type=MESH,
        ).start()
        return carry

    lax.fori_loop(1, GROUP, send_one, 0)

    def send_dec(i, carry):
        t = lax.rem(place + i, GROUP)
        pltpu.make_async_remote_copy(
            dec.at[lax.div(t, GROUP // 2)], dec_in.at[place], dec_sem.at[0], dec_sem.at[1],
            device_id=(fellow(i), head), device_id_type=MESH,
        ).start()
        return carry

    lax.fori_loop(1, GROUP, send_dec, 0)
    pltpu.make_async_copy(state.at[place], pieces.at[place], one_sem.at[1]).start()
    pltpu.make_async_copy(dec.at[lax.div(place, GROUP // 2)], dec_in.at[place], dec_sem.at[1]).start()

    def last_copy(h):
        return pltpu.make_async_remote_copy(
            last.at[h], last_in.at[h], last_sem.at[0, h], last_sem.at[1, h],
            device_id=(lax.rem(seq + 1, nseq), head), device_id_type=MESH,
        )

    @pl.when(inside)
    def _():
        last_copy(0).start()

    w_copy = pltpu.make_async_remote_copy(
        w_hbm, w_sib, wsib_sem.at[0], wsib_sem.at[1], device_id=sibling, device_id_type=MESH
    )
    w_copy.start()

    loads[3].wait()
    for h in range(2):
        cols = pl.ds(h * DH, DH)
        for b in range(2):
            rows = pl.ds(b * BLOCK, BLOCK)
            decay = jnp.exp(jnp.minimum(twice(down[h, b]) - along[h, b], 0.0))
            weights = jnp.where(causal, nt(q[rows, cols], k[rows, cols]) * decay, 0.0).astype(BF16)
            ret[rows, cols] = nn(weights, v[rows, cols])

    @pl.when(crossing)
    def _():
        pl.semaphore_wait(ready_last, 1)
        last_copy(0).start()

    def wait_all(buffer, sem):
        pltpu.make_async_copy(buffer, buffer, sem).wait()

    def wait_sent(buffer, sem):
        most = buffer.at[pl.ds(0, GROUP - 1)]
        pltpu.make_async_copy(most, most, sem).wait()

    wait_all(dec_in, dec_sem.at[1])
    wait_all(pieces, one_sem.at[1])

    so_far, fade_so_far = jnp.zeros((SHARE, DH), F32), jnp.ones((1, 128), F32)
    for n in range(GROUP):
        so_far = so_far * twice(dec_in[n]) + pieces[n].astype(F32)
        fade_so_far = fade_so_far * dec_in[n]
    sums[...] = so_far.astype(BF16)
    fades[...] = fade_so_far

    def sum_copy(source, target):
        return pltpu.make_async_remote_copy(
            sums, sums_in.at[source], sum_send.at[target], sum_recv.at[source],
            device_id=abreast(target), device_id_type=MESH,
        )

    def fade_copy(source, target):
        return pltpu.make_async_remote_copy(
            fades, fades_in.at[source], fade_send.at[target], fade_recv.at[source],
            device_id=abreast(target), device_id_type=MESH,
        )

    def send_sum(other, carry):
        pl.semaphore_wait(ready.at[other], 1)
        sum_copy(group, other).start()
        fade_copy(group, other).start()
        return carry

    lax.fori_loop(group + 1, groups, send_sum, 0)

    @pl.when(jnp.logical_or(inside, crossing))
    def _():
        last_copy(1).start()

    def add_group(other, total_state):
        fade_copy(other, group).wait_recv()
        sum_copy(other, group).wait_recv()
        return total_state * twice(fades_in[other]) + sums_in[other].astype(F32)

    total_state = lax.fori_loop(0, group, add_group, jnp.zeros((SHARE, DH), F32))

    for n in range(GROUP):
        prefixes[n] = total_state.astype(BF16)
        total_state = total_state * twice(dec_in[n]) + pieces[n].astype(F32)

    def send_two(i, carry):
        t = lax.rem(place + i, GROUP)
        pltpu.make_async_remote_copy(
            prefixes.at[t], prior.at[place], two_sem.at[0], two_sem.at[1],
            device_id=(fellow(i), head), device_id_type=MESH,
        ).start()
        return carry

    lax.fori_loop(1, GROUP, send_two, 0)
    pltpu.make_async_copy(prefixes.at[place], prior.at[place], two_sem.at[1]).start()

    loads[4].wait()
    loads[5].wait()
    gate, width = g[...].astype(F32), g.shape[1]
    gated[...] = gain[...].astype(F32).reshape(1, width) * (gate / (1.0 + jnp.exp(-gate)))
    wait_sent(state, one_sem.at[0])
    wait_sent(dec_in, dec_sem.at[0])

    @pl.when(jnp.logical_or(inside, crossing))
    def _():
        last_copy(0).wait_send()
        last_copy(1).wait_send()

    def sums_sent(other, carry):
        sum_copy(group, other).wait_send()
        fade_copy(group, other).wait_send()
        return carry

    lax.fori_loop(group + 1, groups, sums_sent, 0)
    loads[6].wait()

    wait_all(prior, two_sem.at[1])
    def piece(i, c):
        return pl.ds(pl.multiple_of((2 * i + c) * PIECE, PIECE), PIECE)

    def slot(i):
        return pl.ds(pl.multiple_of(lax.rem(i - x + RING, RING) * PIECE, PIECE), PIECE)

    def swap(i):
        return pltpu.make_async_remote_copy(
            hid.at[piece(i, 1 - core)], theirs.at[slot(i)], hid_sem.at[0, i], hid_sem.at[1, i],
            device_id=sibling, device_id_type=MESH,
        )

    per_block = BLOCK // (2 * PIECE)
    for b in range(2):
        rows = pl.ds(b * BLOCK, BLOCK)
        if b == 1:

            @pl.when(seq > 0)
            def _():
                last_copy(0).wait_recv()
                last_copy(1).wait_recv()

            @pl.when(seq == 0)
            def _():
                last_in[...] = jnp.zeros_like(last_in)

        for h in range(2):
            cols = pl.ds(h * DH, DH)
            before = prior[pl.ds(h * (GROUP // 2), GROUP // 2)].reshape(DH, DH)
            if b == 1:
                near_state = last_in[h].astype(F32) * (1.0 - slow_f[h]) + before.astype(F32) * slow_f[h]
                before = (near_state * twice(jnp.exp(total[h, 0])) + first[h]).astype(BF16)
            kept = ret[rows, cols] + nn(q[rows, cols], before) * twice(grow[h, b])
            mean = jnp.mean(kept, axis=1, keepdims=True)
            centered = kept - mean
            var = jnp.mean(centered * centered, axis=1, keepdims=True)
            hid[rows, cols] = (centered * lax.rsqrt(var + 1e-5) * gated[rows, cols]).astype(BF16)
        for i in range(b * per_block, (b + 1) * per_block):
            swap(i).start()
    for i in range(RING):
        mine[slot(i)] = hid[piece(i, core)]
    ahead = nn(mine[...], w[:, :CHUNK])
    w_copy.wait_recv()
    for i in range(RING):
        swap(i).wait_recv()

    def push(kind, j, side, src, dst, to):
        return pltpu.make_async_remote_copy(
            src, dst, p_send.at[kind, j, side], p_recv.at[kind, j, side], device_id=to, device_id_type=MESH
        )

    def far(j, side):
        return push(0, j, side, part.at[j, 2, side], passed.at[j, side], (left, right)[side])

    def near(j, side):
        return push(1, j, side, part.at[j, (1, 3)[side], side], direct.at[j, side], (right, left)[side])

    def onward(j, side):
        return push(2, j, side, part.at[j, (3, 1)[side], side], summed.at[j, side], (left, right)[side])

    def send_parts(j, product):
        product = product.astype(BF16)
        for r in range(RING):
            for side in range(2):
                part[j, r, side] = product[r * PIECE : (r + 1) * PIECE, side * HALF : (side + 1) * HALF]
        far(j, 0).start()
        far(j, 1).start()
        near(j, 0).start()
        near(j, 1).start()

    def project(j, carry):
        cols = pl.ds(pl.multiple_of(j * CHUNK, CHUNK), CHUNK)
        send_parts(j, nn(mine[...], w[:, cols]) + nn(theirs[...], w_sib[:, cols]))
        return carry

    send_parts(0, ahead + nn(theirs[...], w_sib[:, :CHUNK]))
    lax.fori_loop(1, nchunk, project, 0)

    def forward(j, carry):
        for side in range(2):
            far(j, side).wait_recv()
            slot = (3, 1)[side]
            part[j, slot, side] = (part[j, slot, side].astype(F32) + passed[j, side].astype(F32)).astype(BF16)
            onward(j, side).start()
        return carry

    lax.fori_loop(0, nchunk, forward, 0)

    w_copy.wait_send()
    for i in range(RING):
        swap(i).wait_send()
    wait_sent(prefixes, two_sem.at[0])

    def gather(j, carry):
        for side in range(2):
            far(j, side).wait_send()
            near(j, side).wait_send()
            near(j, side).wait_recv()
            own[j, side] = part[j, 0, side].astype(F32) + direct[j, side].astype(F32)
        return carry

    def finish(j, carry):
        for side in range(2):
            onward(j, side).wait_recv()
            cols = pl.ds(pl.multiple_of(j * CHUNK + side * HALF, HALF), HALF)
            out[:, cols] = (own[j, side] + summed[j, side].astype(F32)).astype(BF16)
            onward(j, side).wait_send()
        return carry

    lax.fori_loop(0, nchunk, gather, 0)
    lax.fori_loop(0, nchunk, finish, 0)


def on_device(queries, keys, values, gate, log_decay, trunc_blocks, norm_gain, w_out):
    nseq = lax.axis_size("seq")
    tokens, width = queries.shape
    columns = w_out.shape[1]
    nchunk, groups = columns // CHUNK, nseq // GROUP
    any_spec = pl.BlockSpec(memory_space=pl.ANY)
    vmem, dma = pltpu.VMEM, pltpu.SemaphoreType.DMA
    return pl.pallas_call(
        functools.partial(kernel, nseq, nchunk, tokens // BLOCK * nseq),
        out_shape=pltpu.VMEM((PIECE, columns), BF16),
        in_specs=[any_spec] * 8,
        out_specs=pl.BlockSpec(memory_space=vmem),
        scratch_shapes=[
            vmem((tokens, width), BF16),
            vmem((tokens, width), BF16),
            vmem((tokens, width), BF16),
            vmem((tokens, width), BF16),
            vmem((2, tokens), BF16),
            pltpu.SMEM((2,), jnp.int32),
            vmem((width,), BF16),
            vmem((width, columns), BF16),
            vmem((width, columns), BF16),
            vmem((GROUP, SHARE, DH), BF16),
            vmem((2, DH, DH), F32),
            vmem((2, DH, DH), BF16),
            vmem((2, DH, DH), BF16),
            vmem((2, 1, 128), F32),
            vmem((GROUP, 1, 128), F32),
            vmem((GROUP, SHARE, DH), BF16),
            vmem((GROUP, SHARE, DH), BF16),
            vmem((GROUP, SHARE, DH), BF16),
            vmem((SHARE, DH), BF16),
            vmem((groups, SHARE, DH), BF16),
            vmem((1, 128), F32),
            vmem((groups, 1, 128), F32),
            vmem((tokens, width), F32),
            vmem((tokens, width), F32),
            vmem((2, 2, BLOCK, 128), F32),
            vmem((tokens, width), BF16),
            vmem((RING * PIECE, width), BF16),
            vmem((RING * PIECE, width), BF16),
            vmem((nchunk, RING, 2, PIECE, HALF), BF16),
            vmem((nchunk, 2, PIECE, HALF), BF16),
            vmem((nchunk, 2, PIECE, HALF), BF16),
            vmem((nchunk, 2, PIECE, HALF), BF16),
            vmem((nchunk, 2, PIECE, HALF), F32),
            dma((8,)),
            dma((2,)),
            dma((2,)),
            dma((2,)),
            dma((2, 2)),
            dma((groups,)),
            dma((groups,)),
            dma((groups,)),
            dma((groups,)),
            pltpu.SemaphoreType.REGULAR((groups,)),
            pltpu.SemaphoreType.REGULAR,
            dma((2,)),
            dma((2, RING)),
            dma((3, nchunk, 2)),
            dma((3, nchunk, 2)),
        ],
        compiler_params=pltpu.CompilerParams(
            collective_id=0, has_side_effects=True, vmem_limit_bytes=56 * 2**20
        ),
        cost_estimate=pl.CostEstimate(flops=3 * 10**9, bytes_accessed=7 * 2**20, transcendentals=2**20),
    )(queries, keys, values, gate, log_decay, trunc_blocks, norm_gain, w_out)


def solution(mesh):
    in_specs = (
        P("seq", "head"),
        P("seq", "head"),
        P("seq", "head"),
        P("seq", "head"),
        P("head", "seq"),
        P("head"),
        P("head"),
        P("head", None),
    )
    out_specs = P(("seq", "head"), None)
    return jax.shard_map(on_device, mesh=mesh, in_specs=in_specs, out_specs=out_specs, check_vma=False)
```

```python
import functools

import jax
import jax.numpy as jnp
from jax import lax
from jax.experimental import pallas as pl
from jax.experimental.pallas import tpu as pltpu
from jax.sharding import PartitionSpec as P

MESH = pl.DeviceIdType.MESH
F32 = jnp.float32
BF16 = jnp.bfloat16
BLOCK = 256
DH = 256
CHUNK = 1024
HALF = CHUNK // 2
PIECE = 64
RING = 4
GROUP = 8
SHARE = 2 * DH // GROUP


def nt(a, b):
    return lax.dot_general(a, b, (((1,), (1,)), ((), ())), preferred_element_type=F32)


def tn(a, b):
    return lax.dot_general(a, b, (((0,), (0,)), ((), ())), preferred_element_type=F32)


def nn(a, b):
    return jnp.dot(a, b, preferred_element_type=F32)


def twice(a):
    return jnp.concatenate([a, a], axis=1)


def kernel(
    nseq, nchunk, steps,
    q_hbm, k_hbm, v_hbm, g_hbm, ld_hbm, trunc_hbm, gain_hbm, w_hbm,
    out,
    q, k, v, g, ld, trunc, gain, w, w_sib,
    state, first, last, last_in, dec, dec_in, pieces, prefixes, prior, sums, sums_in, fades, fades_in,
    ret, gated, grow, hid, mine, theirs, part, passed, direct, summed, own,
    load_sem, dec_sem, one_sem, two_sem, last_sem, sum_send, sum_recv, fade_send, fade_recv, ready, ready_last,
    wsib_sem, hid_sem, p_send, p_recv,
):
    seq, head = lax.axis_index("seq"), lax.axis_index("head")
    x, core = lax.div(head, 2), lax.rem(head, 2)
    right = (seq, lax.rem(x + 1, RING) * 2 + core)
    left = (seq, lax.rem(x + RING - 1, RING) * 2 + core)
    sibling = (seq, x * 2 + 1 - core)
    group, place = lax.div(seq, GROUP), lax.rem(seq, GROUP)
    groups = nseq // GROUP
    inside = place < GROUP - 1
    crossing = jnp.logical_and(place == GROUP - 1, group < groups - 1)
    crossed = jnp.logical_and(place == 0, group > 0)

    def fellow(i):
        return group * GROUP + lax.rem(place + i, GROUP)

    def abreast(other):
        return (other * GROUP + place, head)

    barrier = pltpu.get_barrier_semaphore()

    def greet(i, carry):
        pl.semaphore_signal(barrier, inc=1, device_id=(fellow(i), head), device_id_type=MESH)
        return carry

    def greet_later(other, carry):
        pl.semaphore_signal(barrier, inc=1, device_id=abreast(other), device_id_type=MESH)
        return carry

    lax.fori_loop(1, GROUP, greet, 0)
    lax.fori_loop(group + 1, groups, greet_later, 0)

    @pl.when(crossing)
    def _():
        pl.semaphore_signal(barrier, inc=1, device_id=(seq + 1, head), device_id_type=MESH)

    for other in (right, left, sibling):
        pl.semaphore_signal(barrier, inc=1, device_id=other, device_id_type=MESH)

    loads = [
        pltpu.make_async_copy(src, dst, load_sem.at[i])
        for i, (src, dst) in enumerate(
            ((ld_hbm, ld), (k_hbm, k), (v_hbm, v), (q_hbm, q), (g_hbm, g), (gain_hbm, gain), (w_hbm, w), (trunc_hbm, trunc))
        )
    ]
    for copy in loads:
        copy.start()

    loads[7].wait()
    fast = [trunc[h] < steps for h in range(2)]
    slow_f = [jnp.where(f, 0.0, 1.0).astype(F32) for f in fast]
    lower_i = lax.broadcasted_iota(jnp.int32, (BLOCK, BLOCK), 0)
    lower_j = lax.broadcasted_iota(jnp.int32, (BLOCK, BLOCK), 1)
    causal = lower_j <= lower_i
    tri = jnp.where(causal, 1.0, 0.0).astype(BF16)

    loads[0].wait()
    rates = ld[...].astype(F32)
    down, along, total = {}, {}, {}
    for h in range(2):
        for b in range(2):
            row = jnp.broadcast_to(rates[h : h + 1, b * BLOCK : (b + 1) * BLOCK], (128, BLOCK)).astype(BF16)
            down[h, b] = nt(tri, row)
            along[h, b] = nt(row[:16], tri)[:1]
            total[h, b] = down[h, b][BLOCK - 1 :]
            grow[h, b] = jnp.exp(down[h, b])

    loads[1].wait()
    loads[2].wait()
    for h in range(2):
        cols = pl.ds(h * DH, DH)
        states = []
        for b in range(2):
            rows = pl.ds(b * BLOCK, BLOCK)
            fade = twice(jnp.exp(total[h, b] - down[h, b]))
            states.append(tn((k[rows, cols].astype(F32) * fade).astype(BF16), v[rows, cols]))
        whole = states[0] * twice(jnp.exp(total[h, 1])) + states[1]
        state[pl.ds(h * (GROUP // 2), GROUP // 2)] = whole.astype(BF16).reshape(GROUP // 2, SHARE, DH)
        first[h] = states[0]
        last[h] = states[1].astype(BF16)
        dec[h] = jnp.exp(total[h, 0] + total[h, 1]) * slow_f[h]

    pl.semaphore_wait(barrier, GROUP + 2 + group + jnp.where(crossed, 1, 0))

    def send_dec(i, carry):
        t = lax.rem(place + i, GROUP)
        pltpu.make_async_remote_copy(
            dec.at[lax.div(t, GROUP // 2)], dec_in.at[place], dec_sem.at[0], dec_sem.at[1],
            device_id=(fellow(i), head), device_id_type=MESH,
        ).start()
        return carry

    lax.fori_loop(1, GROUP, send_dec, 0)

    def send_one(i, carry):
        t = lax.rem(place + i, GROUP)
        pltpu.make_async_remote_copy(
            state.at[t], pieces.at[place], one_sem.at[0], one_sem.at[1],
            device_id=(fellow(i), head), device_id_type=MESH,
        ).start()
        return carry

    lax.fori_loop(1, GROUP, send_one, 0)

    pltpu.make_async_copy(state.at[place], pieces.at[place], one_sem.at[1]).start()
    pltpu.make_async_copy(dec.at[lax.div(place, GROUP // 2)], dec_in.at[place], dec_sem.at[1]).start()

    def tell(other, carry):
        pl.semaphore_signal(ready.at[group], inc=1, device_id=abreast(other), device_id_type=MESH)
        return carry

    lax.fori_loop(0, group, tell, 0)

    @pl.when(crossed)
    def _():
        pl.semaphore_signal(ready_last, inc=1, device_id=(seq - 1, head), device_id_type=MESH)

    def last_copy(h):
        return pltpu.make_async_remote_copy(
            last.at[h], last_in.at[h], last_sem.at[0, h], last_sem.at[1, h],
            device_id=(lax.rem(seq + 1, nseq), head), device_id_type=MESH,
        )

    @pl.when(inside)
    def _():
        last_copy(0).start()

    w_copy = pltpu.make_async_remote_copy(
        w_hbm, w_sib, wsib_sem.at[0], wsib_sem.at[1], device_id=sibling, device_id_type=MESH
    )
    w_copy.start()

    loads[3].wait()
    for h in range(2):
        cols = pl.ds(h * DH, DH)
        for b in range(2):
            rows = pl.ds(b * BLOCK, BLOCK)
            decay = jnp.exp(jnp.minimum(twice(down[h, b]) - along[h, b], 0.0))
            weights = jnp.where(causal, nt(q[rows, cols], k[rows, cols]) * decay, 0.0).astype(BF16)
            ret[rows, cols] = nn(weights, v[rows, cols])

    @pl.when(crossing)
    def _():
        pl.semaphore_wait(ready_last, 1)
        last_copy(0).start()

    def wait_all(buffer, sem):
        pltpu.make_async_copy(buffer, buffer, sem).wait()

    def wait_sent(buffer, sem):
        most = buffer.at[pl.ds(0, GROUP - 1)]
        pltpu.make_async_copy(most, most, sem).wait()

    wait_all(dec_in, dec_sem.at[1])
    wait_all(pieces, one_sem.at[1])

    so_far, fade_so_far = jnp.zeros((SHARE, DH), F32), jnp.ones((1, 128), F32)
    for n in range(GROUP):
        so_far = so_far * twice(dec_in[n]) + pieces[n].astype(F32)
        fade_so_far = fade_so_far * dec_in[n]
    sums[...] = so_far.astype(BF16)
    fades[...] = fade_so_far

    def sum_copy(source, target):
        return pltpu.make_async_remote_copy(
            sums, sums_in.at[source], sum_send.at[target], sum_recv.at[source],
            device_id=abreast(target), device_id_type=MESH,
        )

    def fade_copy(source, target):
        return pltpu.make_async_remote_copy(
            fades, fades_in.at[source], fade_send.at[target], fade_recv.at[source],
            device_id=abreast(target), device_id_type=MESH,
        )

    def send_sum(other, carry):
        pl.semaphore_wait(ready.at[other], 1)
        sum_copy(group, other).start()
        fade_copy(group, other).start()
        return carry

    lax.fori_loop(group + 1, groups, send_sum, 0)

    @pl.when(jnp.logical_or(inside, crossing))
    def _():
        last_copy(1).start()

    def add_group(other, total_state):
        fade_copy(other, group).wait_recv()
        sum_copy(other, group).wait_recv()
        return total_state * twice(fades_in[other]) + sums_in[other].astype(F32)

    total_state = lax.fori_loop(0, group, add_group, jnp.zeros((SHARE, DH), F32))

    for n in range(GROUP):
        prefixes[n] = total_state.astype(BF16)
        total_state = total_state * twice(dec_in[n]) + pieces[n].astype(F32)

    def send_two(i, carry):
        t = lax.rem(place + i, GROUP)
        pltpu.make_async_remote_copy(
            prefixes.at[t], prior.at[place], two_sem.at[0], two_sem.at[1],
            device_id=(fellow(i), head), device_id_type=MESH,
        ).start()
        return carry

    lax.fori_loop(1, GROUP, send_two, 0)
    pltpu.make_async_copy(prefixes.at[place], prior.at[place], two_sem.at[1]).start()

    loads[4].wait()
    loads[5].wait()
    gate, width = g[...].astype(F32), g.shape[1]
    gated[...] = gain[...].astype(F32).reshape(1, width) * (gate / (1.0 + jnp.exp(-gate)))
    wait_sent(state, one_sem.at[0])
    wait_sent(dec_in, dec_sem.at[0])

    @pl.when(jnp.logical_or(inside, crossing))
    def _():
        last_copy(0).wait_send()
        last_copy(1).wait_send()

    def sums_sent(other, carry):
        sum_copy(group, other).wait_send()
        fade_copy(group, other).wait_send()
        return carry

    lax.fori_loop(group + 1, groups, sums_sent, 0)
    loads[6].wait()

    @pl.when(seq > 0)
    def _():
        last_copy(0).wait_recv()
        last_copy(1).wait_recv()

    @pl.when(seq == 0)
    def _():
        last_in[...] = jnp.zeros_like(last_in)


    wait_all(prior, two_sem.at[1])
    before = {}
    for h in range(2):
        a = prior[pl.ds(h * (GROUP // 2), GROUP // 2)].reshape(DH, DH)
        near_state = last_in[h].astype(F32) * (1.0 - slow_f[h]) + a.astype(F32) * slow_f[h]
        before[h, 0] = a
        before[h, 1] = (near_state * twice(jnp.exp(total[h, 0])) + first[h]).astype(BF16)
    for b in range(2):
        rows = pl.ds(b * BLOCK, BLOCK)
        for h in range(2):
            cols = pl.ds(h * DH, DH)
            kept = ret[rows, cols] + nn(q[rows, cols], before[h, b]) * twice(grow[h, b])
            mean = jnp.mean(kept, axis=1, keepdims=True)
            centered = kept - mean
            var = jnp.mean(centered * centered, axis=1, keepdims=True)
            hid[rows, cols] = (centered * lax.rsqrt(var + 1e-5) * gated[rows, cols]).astype(BF16)

    def rows_of(r, c):
        return pl.ds(pl.multiple_of((lax.rem(x + r, RING) * 2 + c) * PIECE, PIECE), PIECE)

    swaps = []
    for r in range(RING):
        copy = pltpu.make_async_remote_copy(
            hid.at[rows_of(r, 1 - core)], theirs.at[pl.ds(r * PIECE, PIECE)], hid_sem.at[0, r], hid_sem.at[1, r],
            device_id=sibling, device_id_type=MESH,
        )
        copy.start()
        swaps.append(copy)
    for r in range(RING):
        mine[pl.ds(r * PIECE, PIECE)] = hid[rows_of(r, core)]
    w_copy.wait_recv()
    for copy in swaps:
        copy.wait_recv()

    def push(kind, j, side, src, dst, to):
        return pltpu.make_async_remote_copy(
            src, dst, p_send.at[kind, j, side], p_recv.at[kind, j, side], device_id=to, device_id_type=MESH
        )

    def far(j, side):
        return push(0, j, side, part.at[j, 2, side], passed.at[j, side], (left, right)[side])

    def near(j, side):
        return push(1, j, side, part.at[j, (1, 3)[side], side], direct.at[j, side], (right, left)[side])

    def onward(j, side):
        return push(2, j, side, part.at[j, (3, 1)[side], side], summed.at[j, side], (left, right)[side])

    def project(j, carry):
        cols = pl.ds(pl.multiple_of(j * CHUNK, CHUNK), CHUNK)
        product = (nn(mine[...], w[:, cols]) + nn(theirs[...], w_sib[:, cols])).astype(BF16)
        for r in range(RING):
            for side in range(2):
                part[j, r, side] = product[r * PIECE : (r + 1) * PIECE, side * HALF : (side + 1) * HALF]
        far(j, 0).start()
        far(j, 1).start()
        near(j, 0).start()
        near(j, 1).start()
        return carry

    lax.fori_loop(0, nchunk, project, 0)

    def forward(j, carry):
        for side in range(2):
            far(j, side).wait_recv()
            slot = (3, 1)[side]
            part[j, slot, side] = (part[j, slot, side].astype(F32) + passed[j, side].astype(F32)).astype(BF16)
            onward(j, side).start()
        return carry

    lax.fori_loop(0, nchunk, forward, 0)

    w_copy.wait_send()
    for copy in swaps:
        copy.wait_send()
    wait_sent(prefixes, two_sem.at[0])

    def gather(j, carry):
        for side in range(2):
            far(j, side).wait_send()
            near(j, side).wait_send()
            near(j, side).wait_recv()
            own[j, side] = part[j, 0, side].astype(F32) + direct[j, side].astype(F32)
        return carry

    def finish(j, carry):
        for side in range(2):
            onward(j, side).wait_recv()
            cols = pl.ds(pl.multiple_of(j * CHUNK + side * HALF, HALF), HALF)
            out[:, cols] = (own[j, side] + summed[j, side].astype(F32)).astype(BF16)
            onward(j, side).wait_send()
        return carry

    lax.fori_loop(0, nchunk, gather, 0)
    lax.fori_loop(0, nchunk, finish, 0)


def on_device(queries, keys, values, gate, log_decay, trunc_blocks, norm_gain, w_out):
    nseq = lax.axis_size("seq")
    tokens, width = queries.shape
    columns = w_out.shape[1]
    nchunk, groups = columns // CHUNK, nseq // GROUP
    any_spec = pl.BlockSpec(memory_space=pl.ANY)
    vmem, dma = pltpu.VMEM, pltpu.SemaphoreType.DMA
    return pl.pallas_call(
        functools.partial(kernel, nseq, nchunk, tokens // BLOCK * nseq),
        out_shape=pltpu.VMEM((PIECE, columns), BF16),
        in_specs=[any_spec] * 8,
        out_specs=pl.BlockSpec(memory_space=vmem),
        scratch_shapes=[
            vmem((tokens, width), BF16),
            vmem((tokens, width), BF16),
            vmem((tokens, width), BF16),
            vmem((tokens, width), BF16),
            vmem((2, tokens), BF16),
            pltpu.SMEM((2,), jnp.int32),
            vmem((width,), BF16),
            vmem((width, columns), BF16),
            vmem((width, columns), BF16),
            vmem((GROUP, SHARE, DH), BF16),
            vmem((2, DH, DH), F32),
            vmem((2, DH, DH), BF16),
            vmem((2, DH, DH), BF16),
            vmem((2, 1, 128), F32),
            vmem((GROUP, 1, 128), F32),
            vmem((GROUP, SHARE, DH), BF16),
            vmem((GROUP, SHARE, DH), BF16),
            vmem((GROUP, SHARE, DH), BF16),
            vmem((SHARE, DH), BF16),
            vmem((groups, SHARE, DH), BF16),
            vmem((1, 128), F32),
            vmem((groups, 1, 128), F32),
            vmem((tokens, width), F32),
            vmem((tokens, width), F32),
            vmem((2, 2, BLOCK, 128), F32),
            vmem((tokens, width), BF16),
            vmem((RING * PIECE, width), BF16),
            vmem((RING * PIECE, width), BF16),
            vmem((nchunk, RING, 2, PIECE, HALF), BF16),
            vmem((nchunk, 2, PIECE, HALF), BF16),
            vmem((nchunk, 2, PIECE, HALF), BF16),
            vmem((nchunk, 2, PIECE, HALF), BF16),
            vmem((nchunk, 2, PIECE, HALF), F32),
            dma((8,)),
            dma((2,)),
            dma((2,)),
            dma((2,)),
            dma((2, 2)),
            dma((groups,)),
            dma((groups,)),
            dma((groups,)),
            dma((groups,)),
            pltpu.SemaphoreType.REGULAR((groups,)),
            pltpu.SemaphoreType.REGULAR,
            dma((2,)),
            dma((2, RING)),
            dma((3, nchunk, 2)),
            dma((3, nchunk, 2)),
        ],
        compiler_params=pltpu.CompilerParams(
            collective_id=0, has_side_effects=True, vmem_limit_bytes=56 * 2**20
        ),
        cost_estimate=pl.CostEstimate(flops=3 * 10**9, bytes_accessed=7 * 2**20, transcendentals=2**20),
    )(queries, keys, values, gate, log_decay, trunc_blocks, norm_gain, w_out)


def solution(mesh):
    in_specs = (
        P("seq", "head"),
        P("seq", "head"),
        P("seq", "head"),
        P("seq", "head"),
        P("head", "seq"),
        P("head"),
        P("head"),
        P("head", None),
    )
    out_specs = P(("seq", "head"), None)
    return jax.shard_map(on_device, mesh=mesh, in_specs=in_specs, out_specs=out_specs, check_vma=False)
```

```python
import functools

import jax
import jax.numpy as jnp
from jax import lax
from jax.experimental import pallas as pl
from jax.experimental.pallas import tpu as pltpu
from jax.sharding import PartitionSpec as P

MESH = pl.DeviceIdType.MESH
F32 = jnp.float32
BF16 = jnp.bfloat16
BLOCK = 256
DH = 256
CHUNK = 1024
HALF = CHUNK // 2
PIECE = 64
RING = 4
GROUP = 8
SHARE = 2 * DH // GROUP


def nt(a, b):
    return lax.dot_general(a, b, (((1,), (1,)), ((), ())), preferred_element_type=F32)


def tn(a, b):
    return lax.dot_general(a, b, (((0,), (0,)), ((), ())), preferred_element_type=F32)


def nn(a, b):
    return jnp.dot(a, b, preferred_element_type=F32)


def twice(a):
    return jnp.concatenate([a, a], axis=1)


def kernel(
    nseq, nchunk, steps,
    q_hbm, k_hbm, v_hbm, g_hbm, ld_hbm, trunc_hbm, gain_hbm, w_hbm,
    out,
    q, k, v, g, ld, trunc, gain, w, w_sib,
    state, first, last, last_in, dec, dec_in, pieces, prefixes, prior, sums, sums_in, fades, fades_in,
    ret, gated, grow, hid, mine, theirs, part, passed, direct, summed, own,
    load_sem, dec_sem, one_sem, two_sem, last_sem, sum_send, sum_recv, fade_send, fade_recv, ready, ready_last,
    wsib_sem, hid_sem, p_send, p_recv,
):
    seq, head = lax.axis_index("seq"), lax.axis_index("head")
    x, core = lax.div(head, 2), lax.rem(head, 2)
    right = (seq, lax.rem(x + 1, RING) * 2 + core)
    left = (seq, lax.rem(x + RING - 1, RING) * 2 + core)
    sibling = (seq, x * 2 + 1 - core)
    group, place = lax.div(seq, GROUP), lax.rem(seq, GROUP)
    groups = nseq // GROUP
    inside = place < GROUP - 1
    crossing = jnp.logical_and(place == GROUP - 1, group < groups - 1)
    crossed = jnp.logical_and(place == 0, group > 0)

    def fellow(i):
        return group * GROUP + lax.rem(place + i, GROUP)

    def abreast(other):
        return (other * GROUP + place, head)

    barrier = pltpu.get_barrier_semaphore()

    def greet(i, carry):
        pl.semaphore_signal(barrier, inc=1, device_id=(fellow(i), head), device_id_type=MESH)
        return carry

    def greet_later(other, carry):
        pl.semaphore_signal(barrier, inc=1, device_id=abreast(other), device_id_type=MESH)
        return carry

    lax.fori_loop(1, GROUP, greet, 0)
    lax.fori_loop(group + 1, groups, greet_later, 0)

    @pl.when(crossing)
    def _():
        pl.semaphore_signal(barrier, inc=1, device_id=(seq + 1, head), device_id_type=MESH)

    for other in (right, left, sibling):
        pl.semaphore_signal(barrier, inc=1, device_id=other, device_id_type=MESH)

    loads = [
        pltpu.make_async_copy(src, dst, load_sem.at[i])
        for i, (src, dst) in enumerate(
            ((ld_hbm, ld), (k_hbm, k), (v_hbm, v), (q_hbm, q), (g_hbm, g), (gain_hbm, gain), (w_hbm, w), (trunc_hbm, trunc))
        )
    ]
    for copy in loads:
        copy.start()

    loads[7].wait()
    fast = [trunc[h] < steps for h in range(2)]
    slow_f = [jnp.where(f, 0.0, 1.0).astype(F32) for f in fast]
    lower_i = lax.broadcasted_iota(jnp.int32, (BLOCK, BLOCK), 0)
    lower_j = lax.broadcasted_iota(jnp.int32, (BLOCK, BLOCK), 1)
    causal = lower_j <= lower_i
    tri = jnp.where(causal, 1.0, 0.0).astype(BF16)

    loads[0].wait()
    rates = ld[...].astype(F32)
    down, along, total = {}, {}, {}
    for h in range(2):
        for b in range(2):
            row = jnp.broadcast_to(rates[h : h + 1, b * BLOCK : (b + 1) * BLOCK], (128, BLOCK)).astype(BF16)
            down[h, b] = nt(tri, row)
            along[h, b] = nt(row[:16], tri)[:1]
            total[h, b] = down[h, b][BLOCK - 1 :]
            grow[h, b] = jnp.exp(down[h, b])

    loads[1].wait()
    loads[2].wait()
    for h in range(2):
        cols = pl.ds(h * DH, DH)
        states = []
        for b in range(2):
            rows = pl.ds(b * BLOCK, BLOCK)
            fade = twice(jnp.exp(total[h, b] - down[h, b]))
            states.append(tn((k[rows, cols].astype(F32) * fade).astype(BF16), v[rows, cols]))
        whole = states[0] * twice(jnp.exp(total[h, 1])) + states[1]
        state[pl.ds(h * (GROUP // 2), GROUP // 2)] = whole.astype(BF16).reshape(GROUP // 2, SHARE, DH)
        first[h] = states[0]
        last[h] = states[1].astype(BF16)
        dec[h] = jnp.exp(total[h, 0] + total[h, 1]) * slow_f[h]

    pl.semaphore_wait(barrier, GROUP + 2 + group + jnp.where(crossed, 1, 0))

    def send_dec(i, carry):
        t = lax.rem(place + i, GROUP)
        pltpu.make_async_remote_copy(
            dec.at[lax.div(t, GROUP // 2)], dec_in.at[place], dec_sem.at[0], dec_sem.at[1],
            device_id=(fellow(i), head), device_id_type=MESH,
        ).start()
        return carry

    lax.fori_loop(1, GROUP, send_dec, 0)

    def send_one(i, carry):
        t = lax.rem(place + i, GROUP)
        pltpu.make_async_remote_copy(
            state.at[t], pieces.at[place], one_sem.at[0], one_sem.at[1],
            device_id=(fellow(i), head), device_id_type=MESH,
        ).start()
        return carry

    lax.fori_loop(1, GROUP, send_one, 0)

    pltpu.make_async_copy(state.at[place], pieces.at[place], one_sem.at[1]).start()
    pltpu.make_async_copy(dec.at[lax.div(place, GROUP // 2)], dec_in.at[place], dec_sem.at[1]).start()

    def tell(other, carry):
        pl.semaphore_signal(ready.at[group], inc=1, device_id=abreast(other), device_id_type=MESH)
        return carry

    lax.fori_loop(0, group, tell, 0)

    @pl.when(crossed)
    def _():
        pl.semaphore_signal(ready_last, inc=1, device_id=(seq - 1, head), device_id_type=MESH)

    def last_copy(h):
        return pltpu.make_async_remote_copy(
            last.at[h], last_in.at[h], last_sem.at[0, h], last_sem.at[1, h],
            device_id=(lax.rem(seq + 1, nseq), head), device_id_type=MESH,
        )

    @pl.when(inside)
    def _():
        last_copy(0).start()

    w_copy = pltpu.make_async_remote_copy(
        w_hbm, w_sib, wsib_sem.at[0], wsib_sem.at[1], device_id=sibling, device_id_type=MESH
    )
    w_copy.start()

    loads[3].wait()
    for h in range(2):
        cols = pl.ds(h * DH, DH)
        for b in range(2):
            rows = pl.ds(b * BLOCK, BLOCK)
            decay = jnp.exp(jnp.minimum(twice(down[h, b]) - along[h, b], 0.0))
            weights = jnp.where(causal, nt(q[rows, cols], k[rows, cols]) * decay, 0.0).astype(BF16)
            ret[rows, cols] = nn(weights, v[rows, cols])

    @pl.when(crossing)
    def _():
        pl.semaphore_wait(ready_last, 1)
        last_copy(0).start()

    def wait_all(buffer, sem):
        pltpu.make_async_copy(buffer, buffer, sem).wait()

    def wait_sent(buffer, sem):
        most = buffer.at[pl.ds(0, GROUP - 1)]
        pltpu.make_async_copy(most, most, sem).wait()

    wait_all(dec_in, dec_sem.at[1])
    wait_all(pieces, one_sem.at[1])

    so_far, fade_so_far = jnp.zeros((SHARE, DH), F32), jnp.ones((1, 128), F32)
    for n in range(GROUP):
        so_far = so_far * twice(dec_in[n]) + pieces[n].astype(F32)
        fade_so_far = fade_so_far * dec_in[n]
    sums[...] = so_far.astype(BF16)
    fades[...] = fade_so_far

    def sum_copy(source, target):
        return pltpu.make_async_remote_copy(
            sums, sums_in.at[source], sum_send.at[target], sum_recv.at[source],
            device_id=abreast(target), device_id_type=MESH,
        )

    def fade_copy(source, target):
        return pltpu.make_async_remote_copy(
            fades, fades_in.at[source], fade_send.at[target], fade_recv.at[source],
            device_id=abreast(target), device_id_type=MESH,
        )

    def send_sum(other, carry):
        pl.semaphore_wait(ready.at[other], 1)
        fade_copy(group, other).start()
        sum_copy(group, other).start()
        return carry

    lax.fori_loop(group + 1, groups, send_sum, 0)

    @pl.when(jnp.logical_or(inside, crossing))
    def _():
        last_copy(1).start()

    def add_group(other, total_state):
        fade_copy(other, group).wait_recv()
        sum_copy(other, group).wait_recv()
        return total_state * twice(fades_in[other]) + sums_in[other].astype(F32)

    total_state = lax.fori_loop(0, group, add_group, jnp.zeros((SHARE, DH), F32))

    for n in range(GROUP):
        prefixes[n] = total_state.astype(BF16)
        total_state = total_state * twice(dec_in[n]) + pieces[n].astype(F32)

    def send_two(i, carry):
        t = lax.rem(place + i, GROUP)
        pltpu.make_async_remote_copy(
            prefixes.at[t], prior.at[place], two_sem.at[0], two_sem.at[1],
            device_id=(fellow(i), head), device_id_type=MESH,
        ).start()
        return carry

    lax.fori_loop(1, GROUP, send_two, 0)
    pltpu.make_async_copy(prefixes.at[place], prior.at[place], two_sem.at[1]).start()

    loads[4].wait()
    loads[5].wait()
    gate, width = g[...].astype(F32), g.shape[1]
    gated[...] = gain[...].astype(F32).reshape(1, width) * (gate / (1.0 + jnp.exp(-gate)))
    wait_sent(state, one_sem.at[0])
    wait_sent(dec_in, dec_sem.at[0])

    @pl.when(jnp.logical_or(inside, crossing))
    def _():
        last_copy(0).wait_send()
        last_copy(1).wait_send()

    def sums_sent(other, carry):
        sum_copy(group, other).wait_send()
        fade_copy(group, other).wait_send()
        return carry

    lax.fori_loop(group + 1, groups, sums_sent, 0)
    loads[6].wait()

    @pl.when(seq > 0)
    def _():
        last_copy(0).wait_recv()
        last_copy(1).wait_recv()

    @pl.when(seq == 0)
    def _():
        last_in[...] = jnp.zeros_like(last_in)


    wait_all(prior, two_sem.at[1])
    before = {}
    for h in range(2):
        a = prior[pl.ds(h * (GROUP // 2), GROUP // 2)].reshape(DH, DH)
        near_state = last_in[h].astype(F32) * (1.0 - slow_f[h]) + a.astype(F32) * slow_f[h]
        before[h, 0] = a
        before[h, 1] = (near_state * twice(jnp.exp(total[h, 0])) + first[h]).astype(BF16)
    for b in range(2):
        rows = pl.ds(b * BLOCK, BLOCK)
        for h in range(2):
            cols = pl.ds(h * DH, DH)
            kept = ret[rows, cols] + nn(q[rows, cols], before[h, b]) * twice(grow[h, b])
            mean = jnp.mean(kept, axis=1, keepdims=True)
            centered = kept - mean
            var = jnp.mean(centered * centered, axis=1, keepdims=True)
            hid[rows, cols] = (centered * lax.rsqrt(var + 1e-5) * gated[rows, cols]).astype(BF16)

    def rows_of(r, c):
        return pl.ds(pl.multiple_of((lax.rem(x + r, RING) * 2 + c) * PIECE, PIECE), PIECE)

    swaps = []
    for r in range(RING):
        copy = pltpu.make_async_remote_copy(
            hid.at[rows_of(r, 1 - core)], theirs.at[pl.ds(r * PIECE, PIECE)], hid_sem.at[0, r], hid_sem.at[1, r],
            device_id=sibling, device_id_type=MESH,
        )
        copy.start()
        swaps.append(copy)
    for r in range(RING):
        mine[pl.ds(r * PIECE, PIECE)] = hid[rows_of(r, core)]
    w_copy.wait_recv()
    for copy in swaps:
        copy.wait_recv()

    def push(kind, j, side, src, dst, to):
        return pltpu.make_async_remote_copy(
            src, dst, p_send.at[kind, j, side], p_recv.at[kind, j, side], device_id=to, device_id_type=MESH
        )

    def far(j, side):
        return push(0, j, side, part.at[j, 2, side], passed.at[j, side], (left, right)[side])

    def near(j, side):
        return push(1, j, side, part.at[j, (1, 3)[side], side], direct.at[j, side], (right, left)[side])

    def onward(j, side):
        return push(2, j, side, part.at[j, (3, 1)[side], side], summed.at[j, side], (left, right)[side])

    def project(j, carry):
        cols = pl.ds(pl.multiple_of(j * CHUNK, CHUNK), CHUNK)
        product = (nn(mine[...], w[:, cols]) + nn(theirs[...], w_sib[:, cols])).astype(BF16)
        for r in range(RING):
            for side in range(2):
                part[j, r, side] = product[r * PIECE : (r + 1) * PIECE, side * HALF : (side + 1) * HALF]
        far(j, 0).start()
        far(j, 1).start()
        near(j, 0).start()
        near(j, 1).start()
        return carry

    lax.fori_loop(0, nchunk, project, 0)

    def forward(j, carry):
        for side in range(2):
            far(j, side).wait_recv()
            slot = (3, 1)[side]
            part[j, slot, side] = (part[j, slot, side].astype(F32) + passed[j, side].astype(F32)).astype(BF16)
            onward(j, side).start()
        return carry

    lax.fori_loop(0, nchunk, forward, 0)

    w_copy.wait_send()
    for copy in swaps:
        copy.wait_send()
    wait_sent(prefixes, two_sem.at[0])

    def gather(j, carry):
        for side in range(2):
            far(j, side).wait_send()
            near(j, side).wait_send()
            near(j, side).wait_recv()
            own[j, side] = part[j, 0, side].astype(F32) + direct[j, side].astype(F32)
        return carry

    def finish(j, carry):
        for side in range(2):
            onward(j, side).wait_recv()
            cols = pl.ds(pl.multiple_of(j * CHUNK + side * HALF, HALF), HALF)
            out[:, cols] = (own[j, side] + summed[j, side].astype(F32)).astype(BF16)
            onward(j, side).wait_send()
        return carry

    lax.fori_loop(0, nchunk, gather, 0)
    lax.fori_loop(0, nchunk, finish, 0)


def on_device(queries, keys, values, gate, log_decay, trunc_blocks, norm_gain, w_out):
    nseq = lax.axis_size("seq")
    tokens, width = queries.shape
    columns = w_out.shape[1]
    nchunk, groups = columns // CHUNK, nseq // GROUP
    any_spec = pl.BlockSpec(memory_space=pl.ANY)
    vmem, dma = pltpu.VMEM, pltpu.SemaphoreType.DMA
    return pl.pallas_call(
        functools.partial(kernel, nseq, nchunk, tokens // BLOCK * nseq),
        out_shape=pltpu.VMEM((PIECE, columns), BF16),
        in_specs=[any_spec] * 8,
        out_specs=pl.BlockSpec(memory_space=vmem),
        scratch_shapes=[
            vmem((tokens, width), BF16),
            vmem((tokens, width), BF16),
            vmem((tokens, width), BF16),
            vmem((tokens, width), BF16),
            vmem((2, tokens), BF16),
            pltpu.SMEM((2,), jnp.int32),
            vmem((width,), BF16),
            vmem((width, columns), BF16),
            vmem((width, columns), BF16),
            vmem((GROUP, SHARE, DH), BF16),
            vmem((2, DH, DH), F32),
            vmem((2, DH, DH), BF16),
            vmem((2, DH, DH), BF16),
            vmem((2, 1, 128), F32),
            vmem((GROUP, 1, 128), F32),
            vmem((GROUP, SHARE, DH), BF16),
            vmem((GROUP, SHARE, DH), BF16),
            vmem((GROUP, SHARE, DH), BF16),
            vmem((SHARE, DH), BF16),
            vmem((groups, SHARE, DH), BF16),
            vmem((1, 128), F32),
            vmem((groups, 1, 128), F32),
            vmem((tokens, width), F32),
            vmem((tokens, width), F32),
            vmem((2, 2, BLOCK, 128), F32),
            vmem((tokens, width), BF16),
            vmem((RING * PIECE, width), BF16),
            vmem((RING * PIECE, width), BF16),
            vmem((nchunk, RING, 2, PIECE, HALF), BF16),
            vmem((nchunk, 2, PIECE, HALF), BF16),
            vmem((nchunk, 2, PIECE, HALF), BF16),
            vmem((nchunk, 2, PIECE, HALF), BF16),
            vmem((nchunk, 2, PIECE, HALF), F32),
            dma((8,)),
            dma((2,)),
            dma((2,)),
            dma((2,)),
            dma((2, 2)),
            dma((groups,)),
            dma((groups,)),
            dma((groups,)),
            dma((groups,)),
            pltpu.SemaphoreType.REGULAR((groups,)),
            pltpu.SemaphoreType.REGULAR,
            dma((2,)),
            dma((2, RING)),
            dma((3, nchunk, 2)),
            dma((3, nchunk, 2)),
        ],
        compiler_params=pltpu.CompilerParams(
            collective_id=0, has_side_effects=True, vmem_limit_bytes=56 * 2**20
        ),
        cost_estimate=pl.CostEstimate(flops=3 * 10**9, bytes_accessed=7 * 2**20, transcendentals=2**20),
    )(queries, keys, values, gate, log_decay, trunc_blocks, norm_gain, w_out)


def solution(mesh):
    in_specs = (
        P("seq", "head"),
        P("seq", "head"),
        P("seq", "head"),
        P("seq", "head"),
        P("head", "seq"),
        P("head"),
        P("head"),
        P("head", None),
    )
    out_specs = P(("seq", "head"), None)
    return jax.shard_map(on_device, mesh=mesh, in_specs=in_specs, out_specs=out_specs, check_vma=False)
```
